32 devices in a mesh: groups: 2 (over y), rows: 4 (over z), tm: 4 (over x, core).
Axes of the slice: x: 2, y: 2, z: 4, core: 2. Of those that a mesh axis runs over, the one named last changes fastest.
Arguments:
- video: bfloat16 [2, 16, 8, 96, 128], P('groups', 'tm', 'rows'), parts along dimension 0, may hold values from -6 to 6
- gamma_first: float32 [96], replicated, may hold values from 0.25 to 1.75
- kernel_first: bfloat16 [96, 2592], replicated, may hold values from -0.125 to 0.125
- bias_first: float32 [96], replicated, may hold values from -3 to 3
- gamma_second: float32 [96], replicated, may hold values from 0.25 to 1.75
- kernel_second: bfloat16 [96, 2592], replicated, may hold values from -0.125 to 0.125
- bias_second: float32 [96], replicated, may hold values from -3 to 3
Outputs:
- encoded: bfloat16 [2, 16, 8, 96, 128], P('groups', 'tm', 'rows'), parts along dimension 0
The draws below stay inside these ranges and needn't reach their ends.
There are 2 independent parts, one for each index of `groups`. The reference program is written for one: setup_inputs(seed, part) draws one part's arguments, and reference() takes and returns one part's arrays. A program takes and returns all parts, laid end to end along the dimension named above; an argument that names none is the same for every part. Nothing has to cross between parts.
All inputs are finite; a program needn't handle non-finite values.
Results may differ from the reference program's by a relative error of at most 0.0036.
Values may be sent and summed in bfloat16 or wider, within the bound.
No kernel may reach another device: no remote copies, remote signals or barrier semaphores. Data moves between devices by JAX's collectives and lax.ppermute only.
A program may use at most 64 MiB of HBM per device.

```python
import jax
import jax.numpy as jnp
from jax import lax

C = 96
CLIPS = 1
COLS = 128
FRAMES = 16
HEIGHT = 8


def steps_of(key, shape, split, smallest, largest):
    loudness, own = 1.0, jax.random.fold_in(key, 6)
    for dim, parts in split:
        steps = jnp.exp(jax.random.uniform(jax.random.fold_in(own, dim), (parts,), jnp.float32, smallest / len(split), largest / len(split)))
        loudness = loudness * jnp.repeat(steps, shape[dim] // parts).reshape([-1 if axis == dim else 1 for axis in range(len(shape))])
    return loudness


def normal_values(own_key, shape, scale, reach, pieces=(), kind=jnp.bfloat16):
    level = steps_of(own_key, shape, pieces, -0.22, 0.18) if pieces else 1.0
    entries = jax.random.normal(own_key, shape, jnp.float32) * scale * level
    return jnp.minimum(jnp.maximum(entries, -reach), reach).astype(kind)


def setup_inputs(seed: int = 0, part: int = 0) -> dict:
    seeds = jax.random.split(jax.random.key(seed), 8)
    part_splits = jax.random.split(jax.random.fold_in(seeds[7], part), 8)
    return {
        "video": normal_values(part_splits[0], (CLIPS, FRAMES, HEIGHT, C, COLS), 1.0, 6.0, ((1, 4), (2, 4))),
        "gamma_first": jnp.clip(1.0 + 0.15 * jax.random.normal(seeds[1], (C,), jnp.float32), 0.25, 1.75),
        "kernel_first": normal_values(seeds[2], (C, 27 * C), (27 * C) ** -0.5, 0.125),
        "bias_first": normal_values(seeds[3], (C,), 0.5, 3.0, (), jnp.float32),
        "gamma_second": jnp.clip(1.0 + 0.15 * jax.random.normal(seeds[4], (C,), jnp.float32), 0.25, 1.75),
        "kernel_second": normal_values(seeds[5], (C, 27 * C), (27 * C) ** -0.5, 0.125),
        "bias_second": normal_values(seeds[6], (C,), 0.5, 3.0, (), jnp.float32),
    }


epsilon = 1e-06

def norm_silu(values, gain):
    meansq = lax.optimization_barrier(jnp.mean(values * values, axis=3, keepdims=True))
    scaled = values * lax.rsqrt(meansq + epsilon) * gain[:, None]
    return jax.nn.silu(scaled)

def causal_conv(active, kernel, offset):
    clips, frames, height, chans, width = active.shape
    padded = jnp.pad(active, ((0, 0), (2, 0), (1, 1), (0, 0), (1, 1)))
    taps = kernel.astype(jnp.float32).reshape(chans, 3, 3, 3, chans)

    def one_frame(index):
        window = lax.dynamic_slice_in_dim(padded, index, 3, axis=1).astype(jnp.float32)
        summed = jnp.zeros((clips, height, chans, width), jnp.float32)
        for frame_off in range(3):
            for row_off in range(3):
                for col_off in range(3):
                    piece = window[:, frame_off, row_off:row_off + height, :, col_off:col_off + width]
                    summed = summed + jnp.einsum('oc,bhcw->bhow', taps[:, frame_off, row_off, col_off, :], piece, precision=lax.Precision.HIGHEST)
        return summed
    outputs = lax.map(one_frame, jnp.arange(frames, dtype=jnp.int32))
    return jnp.moveaxis(outputs, 0, 1) + offset[:, None]

def reference(video, gamma_first, kernel_first, bias_first, gamma_second, kernel_second, bias_second):
    first = norm_silu(video.astype(jnp.float32), gamma_first).astype(jnp.bfloat16)
    hidden = causal_conv(first, kernel_first, bias_first)
    second = norm_silu(hidden, gamma_second).astype(jnp.bfloat16)
    result = causal_conv(second, kernel_second, bias_second)
    return (video.astype(jnp.float32) + result).astype(jnp.bfloat16)
```

```python
import functools

import jax
import jax.numpy as jnp
from jax import lax
from jax.experimental import pallas as pl
from jax.experimental.pallas import tpu as pltpu
from jax.sharding import PartitionSpec as P

epsilon = 1e-06
VMEM = pl.BlockSpec(memory_space=pltpu.VMEM)
SMEM = pl.BlockSpec(memory_space=pltpu.SMEM)


def column(vector_ref):
    row = vector_ref[...].reshape(1, -1)
    count = row.shape[1]
    down = lax.broadcasted_iota(jnp.int32, (count, count), 0)
    across = lax.broadcasted_iota(jnp.int32, (count, count), 1)
    return jnp.sum(jnp.where(down == across, row, 0.0), axis=1, keepdims=True)


def norm_silu(values, gain):
    meansq = jnp.mean(values * values, axis=-2, keepdims=True)
    half = values * lax.rsqrt(meansq + epsilon) * (0.5 * gain)
    return half + half * jnp.tanh(half)


def restacked(weights, frame_offs):
    chans = weights.shape[0]
    return jnp.concatenate(
        [
            jnp.concatenate(
                [
                    weights[:, (m * 3 + k) * chans : (m * 3 + k + 1) * chans]
                    for m in range(3 * frame_offs[0], 3 * frame_offs[1])
                ],
                axis=1,
            )
            for k in range(3)
        ],
        axis=0,
    )


def conv_two_rows(weights, cells, frame, count, row):
    chans, width = cells.shape[2:]
    depth = 3 * count * chans
    windows = jnp.concatenate(
        [
            cells[frame : frame + count, row : row + 3].reshape(depth, width),
            cells[frame : frame + count, row + 1 : row + 4].reshape(depth, width),
        ],
        axis=1,
    )
    stacked = jnp.dot(weights, windows, preferred_element_type=jnp.float32)
    lane = lax.broadcasted_iota(jnp.int32, (chans, width), 1)
    sums = []
    for side in range(2):
        part = stacked[:, side * width : (side + 1) * width]
        left = jnp.where(lane == 0, 0.0, pltpu.roll(part[:chans], 1, 1))
        right = jnp.where(lane == width - 1, 0.0, pltpu.roll(part[2 * chans :], width - 1, 1))
        sums.append(part[chans : 2 * chans] + left + right)
    return sums


def fill_active(active, blocks, gain):
    row = 0
    for block in blocks:
        for frame in range(block.shape[1]):
            for inner in range(block.shape[2]):
                values = block[0, frame, inner].astype(jnp.float32)
                active[frame, row + inner] = norm_silu(values, gain).astype(jnp.bfloat16)
        row += block.shape[2]


def own_kernel(
    edge, video, above, below, gamma_first, kernel_first, bias_first, gamma_second, kernel_second,
    partial, second, first_0, first_01, first_all, second_all, active,
):
    weights = kernel_first[...]
    stacked_all = restacked(weights, (0, 3))
    first_all[...] = stacked_all
    first_0[...] = restacked(weights, (0, 1))
    first_01[...] = restacked(weights, (0, 2))
    second_all[...] = restacked(kernel_second[...], (0, 3))
    stacked_2 = restacked(weights, (2, 3))
    stacked_12 = restacked(weights, (1, 3))
    fill_active(active, (above, video, below), column(gamma_first))
    bias = column(bias_first)
    gain = column(gamma_second)
    frames = video.shape[1]
    for frame in range(frames):
        for row in (0, 2):
            if frame == 0:
                sums = conv_two_rows(stacked_2, active, 0, 1, row)
            elif frame == 1:
                sums = conv_two_rows(stacked_12, active, 0, 2, row)
            else:
                sums = conv_two_rows(first_all[...], active, frame - 2, 3, row)
            for side in range(2):
                hidden = sums[side] + bias
                if frame < 2:
                    partial[frame, row + side] = hidden
                else:
                    value = norm_silu(hidden, gain)
                    if row + side == 0:
                        value = value * edge[0]
                    if row + side == 3:
                        value = value * edge[1]
                    second[frame - 2, row + side] = value.astype(jnp.bfloat16)


def last_kernel(
    edge, video, prior, above, below, partial, late, first_0, first_01, first_all, second_all,
    gamma_first, bias_first, gamma_second, bias_second, encoded, active, second,
):
    fill_active(active, (above, prior, below), column(gamma_first))
    bias = column(bias_first)
    gain = column(gamma_second)
    frames = video.shape[1]
    second[4 : frames + 2] = late[...]
    for frame in range(4):
        for row in (0, 2):
            if frame < 2:
                sums = conv_two_rows(first_all[...], active, frames - 4 + frame, 3, row)
            elif frame == 2:
                sums = conv_two_rows(first_01[...], active, frames - 2, 2, row)
            else:
                sums = conv_two_rows(first_0[...], active, frames - 1, 1, row)
            for side in range(2):
                if frame < 2:
                    value = norm_silu(sums[side] + bias, gain) * edge[2]
                else:
                    value = norm_silu(sums[side] + partial[frame - 2, row + side], gain)
                if row + side == 0:
                    value = value * edge[0]
                if row + side == 3:
                    value = value * edge[1]
                second[frame, row + side] = value.astype(jnp.bfloat16)
    offset = column(bias_second)
    for frame in range(frames):
        sums = conv_two_rows(second_all[...], second, frame, 3, 0)
        for side in range(2):
            value = video[0, frame, side].astype(jnp.float32) + (sums[side] + offset)
            encoded[0, frame, side] = value.astype(jnp.bfloat16)


def from_neighbour(block, frame_step, row_step):
    frame_parts, row_parts = lax.axis_size("tm"), lax.axis_size("rows")
    route = []
    for row in range(row_parts):
        for part in range(frame_parts):
            row_to, part_to = row + row_step, part + frame_step
            if 0 <= row_to < row_parts and 0 <= part_to < frame_parts:
                route.append((row * frame_parts + part, row_to * frame_parts + part_to))
    return lax.ppermute(block, ("rows", "tm"), route)


def local(video, gamma_first, kernel_first, bias_first, gamma_second, kernel_second, bias_second):
    _, frames, rows, chans, width = video.shape
    above = from_neighbour(video, 0, 1)
    below = from_neighbour(video, 0, -1)
    prior_above = from_neighbour(video, 1, 1)
    prior_below = from_neighbour(video, 1, -1)
    prior = from_neighbour(video, 1, 0)
    row_part = lax.axis_index("rows")
    edge = jnp.stack(
        [row_part > 0, row_part < lax.axis_size("rows") - 1, lax.axis_index("tm") > 0]
    ).astype(jnp.float32)
    bf16, f32 = jnp.bfloat16, jnp.float32
    shape = jax.ShapeDtypeStruct
    params = pltpu.CompilerParams(vmem_limit_bytes=24 * 2**20)
    partial, late, first_0, first_01, first_all, second_all = pl.pallas_call(
        own_kernel,
        out_shape=(
            shape((2, rows + 2, chans, width), f32),
            shape((frames - 2, rows + 2, chans, width), bf16),
            shape((3 * chans, 3 * chans), bf16),
            shape((3 * chans, 6 * chans), bf16),
            shape((3 * chans, 9 * chans), bf16),
            shape((3 * chans, 9 * chans), bf16),
        ),
        in_specs=[SMEM] + [VMEM] * 8,
        out_specs=[VMEM] * 6,
        scratch_shapes=[pltpu.VMEM((frames, rows + 4, chans, width), bf16)],
        compiler_params=params,
        cost_estimate=pl.CostEstimate(flops=2 * 10**9, bytes_accessed=4 * 10**6, transcendentals=10**6),
    )(edge, video, above, below, gamma_first, kernel_first, bias_first, gamma_second, kernel_second)
    return pl.pallas_call(
        last_kernel,
        out_shape=shape(video.shape, bf16),
        in_specs=[SMEM] + [VMEM] * 14,
        out_specs=VMEM,
        scratch_shapes=[
            pltpu.VMEM((frames, rows + 4, chans, width), bf16),
            pltpu.VMEM((frames + 2, rows + 2, chans, width), bf16),
        ],
        compiler_params=params,
        cost_estimate=pl.CostEstimate(flops=2 * 10**9, bytes_accessed=4 * 10**6, transcendentals=10**6),
    )(
        edge, video, prior, prior_above, prior_below, partial, late, first_0, first_01, first_all, second_all,
        gamma_first, bias_first, gamma_second, bias_second,
    )


def solution(mesh):
    in_specs = (P("groups", "tm", "rows", None, None), P(), P(), P(), P(), P(), P())
    out_specs = P("groups", "tm", "rows", None, None)
    return jax.shard_map(local, mesh=mesh, in_specs=in_specs, out_specs=out_specs, check_vma=False)
```

```python
import jax
import jax.numpy as jnp
from jax import lax
from jax.experimental import pallas as pl
from jax.experimental.pallas import tpu as pltpu
from jax.sharding import PartitionSpec as P

epsilon = 1e-06
VMEM = pl.BlockSpec(memory_space=pltpu.VMEM)


def column(vector_ref):
    row = vector_ref[...].reshape(1, -1)
    count = row.shape[1]
    down = lax.broadcasted_iota(jnp.int32, (count, count), 0)
    across = lax.broadcasted_iota(jnp.int32, (count, count), 1)
    return jnp.sum(jnp.where(down == across, row, 0.0), axis=1, keepdims=True)


def norm_silu(values, gain):
    meansq = jnp.mean(values * values, axis=-2, keepdims=True)
    half = values * lax.rsqrt(meansq + epsilon) * (0.5 * gain)
    return half + half * jnp.tanh(half)


def activate(block, out, gain):
    for frame in range(block.shape[1]):
        for row in range(block.shape[2]):
            values = block[0, frame, row].astype(jnp.float32)
            out[frame, row] = norm_silu(values, gain).astype(jnp.bfloat16)


def restack(weights, out, padded):
    chans = weights.shape[0]
    blank = jnp.zeros((chans, chans), weights.dtype)
    for k in range(3):
        pieces = []
        for i in range(3):
            for j in range(3):
                start = ((i * 3 + j) * 3 + k) * chans
                pieces.append(weights[:, start : start + chans])
            if padded:
                pieces.append(blank)
        out[k * chans : (k + 1) * chans, :] = jnp.concatenate(pieces, axis=1)


def conv_two_rows(weights, rows, frame, count, padded):
    halves = []
    for side in range(2):
        pieces = []
        for offset in range(frame, frame + count):
            for cells, row in rows[side : side + 3] + (rows[side + 1 : side + 2] if padded else []):
                pieces.append(cells[offset, row])
        halves.append(jnp.concatenate(pieces, axis=0))
    stacked = jnp.dot(weights, jnp.concatenate(halves, axis=1), preferred_element_type=jnp.float32)
    chans, width = pieces[0].shape
    lane = lax.broadcasted_iota(jnp.int32, (chans, width), 1)
    sums = []
    for side in range(2):
        part = stacked[:, side * width : (side + 1) * width]
        left = jnp.where(lane == 0, 0.0, pltpu.roll(part[:chans], 1, 1))
        right = jnp.where(lane == width - 1, 0.0, pltpu.roll(part[2 * chans :], width - 1, 1))
        sums.append(part[chans : 2 * chans] + left + right)
    return sums


def row_pairs(top, bottom):
    return [(top, 0), (top, 1), (bottom, 0), (bottom, 1)]


def either_way(flag, near, own, body):
    @pl.when(~flag)
    def _():
        body(row_pairs(near, own))

    @pl.when(flag)
    def _():
        body(row_pairs(own, near))


def own_kernel(video, gamma_first, bias_first, gamma_second, bias_second, own, columns):
    for index, vector in enumerate((gamma_first, bias_first, gamma_second, bias_second)):
        columns[index] = jnp.broadcast_to(column(vector), columns.shape[1:])
    activate(video, own, columns[0])


def even_partner_below():
    return lax.rem(lax.axis_index("rows"), 2) == 0


def edge_kernel(valid):
    row_part = lax.axis_index("rows")
    one_below = even_partner_below()
    has_above = row_part > 0
    has_below = row_part < lax.axis_size("rows") - 1
    inside = (
        has_above | one_below,
        has_below | ~one_below,
        has_above | ~one_below,
        has_below | one_below,
        lax.axis_index("tm") > 0,
    )
    for index, flag in enumerate(inside):
        valid[index] = jnp.broadcast_to(jnp.where(flag, 1.0, 0.0), valid.shape[1:])


def present_frames(rows, first, columns, valid, base, partial, late):
    bias, gain = columns[1], columns[2]
    depth = first.shape[1] // 3
    frames = late.shape[0] + 2
    for frame in range(frames):
        count = min(frame + 1, 3)
        sums = conv_two_rows(first[:, (3 - count) * depth :], rows, frame + 1 - count, count, True)
        for side in range(2):
            hidden = sums[side] + bias
            if frame < 2:
                partial[frame, side] = hidden
            else:
                late[frame - 2, side] = (norm_silu(hidden, gain) * valid[base + side, 0:1]).astype(jnp.bfloat16)


def earlier_frames(rows, first, columns, valid, base, partial, early):
    bias, gain = columns[1], columns[2]
    depth = first.shape[1] // 3
    frames = rows[0][0].shape[0]
    for frame in range(4):
        count = min(3, 4 - frame)
        sums = conv_two_rows(first[:, : count * depth], rows, frames - 4 + frame, count, True)
        for side in range(2):
            if frame < 2:
                value = norm_silu(sums[side] + bias, gain) * valid[4, 0:1]
            else:
                value = norm_silu(sums[side] + partial[frame - 2, side], gain)
            early[frame, side] = (value * valid[base + side, 0:1]).astype(jnp.bfloat16)


def one_kernel(
    valid, one, own, kernel_first, kernel_second, columns,
    first, second, partial, late, active,
):
    one_below = even_partner_below()
    activate(one, active, columns[0])
    restack(kernel_first[...], first, True)
    restack(kernel_second[...], second, False)
    either_way(
        one_below, active, own, lambda rows: present_frames(rows, first, columns, valid, 0, partial, late)
    )


def two_kernel(
    valid, two, prior, prior_one, own, first, columns, partial_one,
    inner, partial, late, early, active, active_prior,
):
    one_below = even_partner_below()
    activate(two, active, columns[0])
    either_way(
        ~one_below, active, own, lambda rows: present_frames(rows, first, columns, valid, 2, partial, late)
    )
    activate(prior, inner, columns[0])
    activate(prior_one, active_prior, columns[0])
    either_way(
        one_below, active_prior, inner,
        lambda rows: earlier_frames(rows, first, columns, valid, 0, partial_one, early),
    )


def last_kernel(
    valid, video, prior_two, inner, first, second, columns, early_one, late_one, partial_two, late_two,
    encoded, active, near_one, near_two,
):
    one_below = even_partner_below()
    activate(prior_two, active, columns[0])
    near_one[0:4] = early_one[...]
    near_one[4:] = late_one[...]
    near_two[4:] = late_two[...]
    either_way(
        ~one_below, active, inner,
        lambda rows: earlier_frames(rows, first, columns, valid, 2, partial_two, near_two),
    )
    offset = columns[3]

    def finish(rows):
        for frame in range(video.shape[1]):
            sums = conv_two_rows(second[...], rows, frame, 3, False)
            for side in range(2):
                value = video[0, frame, side].astype(jnp.float32) + (sums[side] + offset)
                encoded[0, frame, side] = value.astype(jnp.bfloat16)

    either_way(one_below, near_one, near_two, finish)


def routed(block, goal):
    frame_parts, row_parts = lax.axis_size("tm"), lax.axis_size("rows")
    route = []
    for row in range(row_parts):
        for part in range(frame_parts):
            row_to, part_to = goal(row, part)
            if 0 <= row_to < row_parts and 0 <= part_to < frame_parts:
                route.append((row * frame_parts + part, row_to * frame_parts + part_to))
    return lax.ppermute(block, ("rows", "tm"), route)


def later(row, part):
    return row, part + 1


def even_pair(row, part):
    return row + 1 - 2 * (row % 2), part


def odd_pair(row, part):
    return row - 1 + 2 * (row % 2), part


def exchange(video):
    prior = routed(video, later)
    two = routed(video, odd_pair)
    one = routed(video, even_pair)
    prior_two = routed(prior, odd_pair)
    prior_one = routed(prior, even_pair)
    return one, two, prior, prior_one, prior_two


def local(video, gamma_first, kernel_first, bias_first, gamma_second, kernel_second, bias_second):
    _, frames, rows, chans, width = video.shape
    one, two, prior, prior_one, prior_two = exchange(video)
    bf16, f32 = jnp.bfloat16, jnp.float32
    shape = jax.ShapeDtypeStruct
    params = pltpu.CompilerParams(vmem_limit_bytes=24 * 2**20)

    def cost(millions):
        return pl.CostEstimate(flops=millions * 10**6, bytes_accessed=10**6, transcendentals=10**5)

    block = shape((frames, rows, chans, width), bf16)
    pair = shape((2, 2, chans, width), f32)
    late = shape((frames - 2, 2, chans, width), bf16)
    early = shape((4, 2, chans, width), bf16)
    in_vmem = pltpu.VMEM(block.shape, bf16)
    valid = pl.pallas_call(
        edge_kernel,
        out_shape=shape((5, 8, width), f32),
        out_specs=VMEM,
        compiler_params=params,
        cost_estimate=cost(2000),
    )()
    own, columns = pl.pallas_call(
        own_kernel,
        out_shape=(block, shape((4, chans, width), f32)),
        in_specs=[VMEM] * 5,
        out_specs=[VMEM] * 2,
        compiler_params=params,
        cost_estimate=cost(1000),
    )(video, gamma_first, bias_first, gamma_second, bias_second)
    first, second, partial_one, late_one = pl.pallas_call(
        one_kernel,
        out_shape=(shape((3 * chans, 12 * chans), bf16), shape((3 * chans, 9 * chans), bf16), pair, late),
        in_specs=[VMEM] * 6,
        out_specs=[VMEM] * 4,
        scratch_shapes=[in_vmem],
        compiler_params=params,
        cost_estimate=cost(1000),
    )(valid, one, own, kernel_first, kernel_second, columns)
    inner, partial_two, late_two, early_one = pl.pallas_call(
        two_kernel,
        out_shape=(block, pair, late, early),
        in_specs=[VMEM] * 8,
        out_specs=[VMEM] * 4,
        scratch_shapes=[in_vmem, in_vmem],
        compiler_params=params,
        cost_estimate=cost(1000),
    )(valid, two, prior, prior_one, own, first, columns, partial_one)
    return pl.pallas_call(
        last_kernel,
        out_shape=shape(video.shape, bf16),
        in_specs=[VMEM] * 11,
        out_specs=VMEM,
        scratch_shapes=[in_vmem] + [pltpu.VMEM((frames + 2, 2, chans, width), bf16)] * 2,
        compiler_params=params,
        cost_estimate=cost(1000),
    )(valid, video, prior_two, inner, first, second, columns, early_one, late_one, partial_two, late_two)


def solution(mesh):
    in_specs = (P("groups", "tm", "rows", None, None), P(), P(), P(), P(), P(), P())
    out_specs = P("groups", "tm", "rows", None, None)
    return jax.shard_map(local, mesh=mesh, in_specs=in_specs, out_specs=out_specs, check_vma=False)
```

```python
import jax
import jax.numpy as jnp
from jax import lax
from jax.experimental import pallas as pl
from jax.experimental.pallas import tpu as pltpu
from jax.sharding import PartitionSpec as P

epsilon = 1e-06
VMEM = pl.BlockSpec(memory_space=pltpu.VMEM)


def column(vector_ref):
    row = vector_ref[...].reshape(1, -1)
    count = row.shape[1]
    down = lax.broadcasted_iota(jnp.int32, (count, count), 0)
    across = lax.broadcasted_iota(jnp.int32, (count, count), 1)
    return jnp.sum(jnp.where(down == across, row, 0.0), axis=1, keepdims=True)


def norm_silu(values, gain):
    meansq = jnp.mean(values * values, axis=-2, keepdims=True)
    half = values * lax.rsqrt(meansq + epsilon) * (0.5 * gain)
    return half + half * jnp.tanh(half)


def activate(block, out, gain):
    for frame in range(block.shape[1]):
        for row in range(block.shape[2]):
            values = block[0, frame, row].astype(jnp.float32)
            out[frame, row] = norm_silu(values, gain).astype(jnp.bfloat16)


def restack(weights, out, padded):
    chans = weights.shape[0]
    blank = jnp.zeros((chans, chans), weights.dtype)
    for k in range(3):
        pieces = []
        for i in range(3):
            for j in range(3):
                start = ((i * 3 + j) * 3 + k) * chans
                pieces.append(weights[:, start : start + chans])
            if padded:
                pieces.append(blank)
        out[k * chans : (k + 1) * chans, :] = jnp.concatenate(pieces, axis=1)


def conv_two_rows(weights, rows, frame, count, padded):
    halves = []
    for side in range(2):
        pieces = []
        for offset in range(frame, frame + count):
            for cells, row in rows[side : side + 3] + (rows[side + 1 : side + 2] if padded else []):
                pieces.append(cells[offset, row])
        halves.append(jnp.concatenate(pieces, axis=0))
    stacked = jnp.dot(weights, jnp.concatenate(halves, axis=1), preferred_element_type=jnp.float32)
    chans, width = pieces[0].shape
    lane = lax.broadcasted_iota(jnp.int32, (chans, width), 1)
    sums = []
    for side in range(2):
        part = stacked[:, side * width : (side + 1) * width]
        left = jnp.where(lane == 0, 0.0, pltpu.roll(part[:chans], 1, 1))
        right = jnp.where(lane == width - 1, 0.0, pltpu.roll(part[2 * chans :], width - 1, 1))
        sums.append(part[chans : 2 * chans] + left + right)
    return sums


def row_pairs(top, bottom):
    return [(top, 0), (top, 1), (bottom, 0), (bottom, 1)]


def either_way(flag, near, own, body):
    @pl.when(~flag)
    def _():
        body(row_pairs(near, own))

    @pl.when(flag)
    def _():
        body(row_pairs(own, near))


def own_kernel(video, gamma_first, bias_first, gamma_second, bias_second, own, columns):
    for index, vector in enumerate((gamma_first, bias_first, gamma_second, bias_second)):
        columns[index] = jnp.broadcast_to(column(vector), columns.shape[1:])
    activate(video, own, columns[0])


def even_partner_below():
    return lax.rem(lax.axis_index("rows"), 2) == 0


def edge_kernel(valid):
    row_part = lax.axis_index("rows")
    one_below = even_partner_below()
    has_above = row_part > 0
    has_below = row_part < lax.axis_size("rows") - 1
    later = lax.axis_index("tm") > 0
    has_one = (one_below & has_below) | (~one_below & has_above)
    has_two = (one_below & has_above) | (~one_below & has_below)
    inside = (
        has_above | one_below,
        has_below | ~one_below,
        has_above | ~one_below,
        has_below | one_below,
        later,
        has_one,
        has_two,
        later & has_one,
        later & has_two,
    )
    for index, flag in enumerate(inside):
        valid[index] = jnp.broadcast_to(jnp.where(flag, 1.0, 0.0), valid.shape[1:])


def present_frames(rows, first, columns, valid, base, partial, late):
    bias, gain = columns[1], columns[2]
    depth = first.shape[1] // 3
    frames = late.shape[0] + 2
    for frame in range(frames):
        count = min(frame + 1, 3)
        sums = conv_two_rows(first[:, (3 - count) * depth :], rows, frame + 1 - count, count, True)
        for side in range(2):
            hidden = sums[side] + bias
            if frame < 2:
                partial[frame, side] = hidden
            else:
                late[frame - 2, side] = (norm_silu(hidden, gain) * valid[base + side, 0:1]).astype(jnp.bfloat16)


def earlier_frames(rows, first, columns, valid, base, partial, early):
    bias, gain = columns[1], columns[2]
    depth = first.shape[1] // 3
    frames = rows[0][0].shape[0]
    for frame in range(4):
        count = min(3, 4 - frame)
        sums = conv_two_rows(first[:, : count * depth], rows, frames - 4 + frame, count, True)
        for side in range(2):
            if frame < 2:
                value = norm_silu(sums[side] + bias, gain) * valid[4, 0:1]
            else:
                value = norm_silu(sums[side] + partial[frame - 2, side], gain)
            early[frame, side] = (value * valid[base + side, 0:1]).astype(jnp.bfloat16)


def one_kernel(
    valid, one, own, kernel_first, kernel_second, columns,
    first, second, partial, late, active,
):
    one_below = even_partner_below()
    activate(one, active, columns[0] * valid[5, 0:1])
    restack(kernel_first[...], first, True)
    restack(kernel_second[...], second, False)
    either_way(
        one_below, active, own, lambda rows: present_frames(rows, first, columns, valid, 0, partial, late)
    )


def two_kernel(valid, two, prior, own, first, columns, inner, partial, late, active):
    one_below = even_partner_below()
    activate(two, active, columns[0] * valid[6, 0:1])
    activate(prior, inner, columns[0] * valid[4, 0:1])
    either_way(
        ~one_below, active, own, lambda rows: present_frames(rows, first, columns, valid, 2, partial, late)
    )


def prior_kernel(valid, prior_one, inner, first, columns, partial, early, active):
    one_below = even_partner_below()
    activate(prior_one, active, columns[0] * valid[7, 0:1])
    either_way(
        one_below, active, inner, lambda rows: earlier_frames(rows, first, columns, valid, 0, partial, early)
    )


def last_kernel(
    valid, video, prior_two, inner, first, second, columns, early_one, late_one, partial_two, late_two,
    encoded, active, near_one, near_two,
):
    one_below = even_partner_below()
    activate(prior_two, active, columns[0] * valid[8, 0:1])
    near_one[0:4] = early_one[...]
    near_one[4:] = late_one[...]
    near_two[4:] = late_two[...]
    either_way(
        ~one_below, active, inner,
        lambda rows: earlier_frames(rows, first, columns, valid, 2, partial_two, near_two),
    )
    offset = columns[3]

    def finish(rows):
        for frame in range(video.shape[1]):
            sums = conv_two_rows(second[...], rows, frame, 3, False)
            for side in range(2):
                value = video[0, frame, side].astype(jnp.float32) + (sums[side] + offset)
                encoded[0, frame, side] = value.astype(jnp.bfloat16)

    either_way(one_below, near_one, near_two, finish)


def routed(block, goal):
    row_parts, frame_parts = lax.axis_size("rows"), lax.axis_size("tm")
    route = []
    for row in range(row_parts):
        for part in range(frame_parts):
            row_to, part_to = goal(row, part, row_parts, frame_parts)
            route.append((row * frame_parts + part, row_to * frame_parts + part_to))
    return lax.ppermute(block, ("rows", "tm"), route)


def later(row, part, row_parts, frame_parts):
    return row, (part + 1) % frame_parts


def paired(row, part, partner, row_parts, frame_parts):
    if 0 <= partner < row_parts:
        return partner, part
    return row, min(part ^ 1, frame_parts - 1)


def even_pair(row, part, row_parts, frame_parts):
    return paired(row, part, row + 1 - 2 * (row % 2), row_parts, frame_parts)


def odd_pair(row, part, row_parts, frame_parts):
    return paired(row, part, row - 1 + 2 * (row % 2), row_parts, frame_parts)


def exchange(video):
    prior = routed(video, later)
    two = routed(video, odd_pair)
    one = routed(video, even_pair)
    prior_two = routed(prior, odd_pair)
    prior_one = routed(prior, even_pair)
    return one, two, prior, prior_one, prior_two


def local(video, gamma_first, kernel_first, bias_first, gamma_second, kernel_second, bias_second):
    _, frames, rows, chans, width = video.shape
    one, two, prior, prior_one, prior_two = exchange(video)
    bf16, f32 = jnp.bfloat16, jnp.float32
    shape = jax.ShapeDtypeStruct
    params = pltpu.CompilerParams(vmem_limit_bytes=24 * 2**20)

    def cost(millions):
        return pl.CostEstimate(flops=millions * 10**6, bytes_accessed=10**6, transcendentals=10**5)

    block = shape((frames, rows, chans, width), bf16)
    pair = shape((2, 2, chans, width), f32)
    late = shape((frames - 2, 2, chans, width), bf16)
    early = shape((4, 2, chans, width), bf16)
    in_vmem = pltpu.VMEM(block.shape, bf16)
    valid = pl.pallas_call(
        edge_kernel,
        out_shape=shape((9, 8, width), f32),
        out_specs=VMEM,
        compiler_params=params,
        cost_estimate=cost(2000),
    )()
    own, columns = pl.pallas_call(
        own_kernel,
        out_shape=(block, shape((4, chans, width), f32)),
        in_specs=[VMEM] * 5,
        out_specs=[VMEM] * 2,
        compiler_params=params,
        cost_estimate=cost(1000),
    )(video, gamma_first, bias_first, gamma_second, bias_second)
    first, second, partial_one, late_one = pl.pallas_call(
        one_kernel,
        out_shape=(shape((3 * chans, 12 * chans), bf16), shape((3 * chans, 9 * chans), bf16), pair, late),
        in_specs=[VMEM] * 6,
        out_specs=[VMEM] * 4,
        scratch_shapes=[in_vmem],
        compiler_params=params,
        cost_estimate=cost(1000),
    )(valid, one, own, kernel_first, kernel_second, columns)
    inner, partial_two, late_two = pl.pallas_call(
        two_kernel,
        out_shape=(block, pair, late),
        in_specs=[VMEM] * 6,
        out_specs=[VMEM] * 3,
        scratch_shapes=[in_vmem],
        compiler_params=params,
        cost_estimate=cost(1000),
    )(valid, two, prior, own, first, columns)
    early_one = pl.pallas_call(
        prior_kernel,
        out_shape=early,
        in_specs=[VMEM] * 6,
        out_specs=VMEM,
        scratch_shapes=[in_vmem],
        compiler_params=params,
        cost_estimate=cost(1000),
    )(valid, prior_one, inner, first, columns, partial_one)
    return pl.pallas_call(
        last_kernel,
        out_shape=shape(video.shape, bf16),
        in_specs=[VMEM] * 11,
        out_specs=VMEM,
        scratch_shapes=[in_vmem] + [pltpu.VMEM((frames + 2, 2, chans, width), bf16)] * 2,
        compiler_params=params,
        cost_estimate=cost(1000),
    )(valid, video, prior_two, inner, first, second, columns, early_one, late_one, partial_two, late_two)


def solution(mesh):
    in_specs = (P("groups", "tm", "rows", None, None), P(), P(), P(), P(), P(), P())
    out_specs = P("groups", "tm", "rows", None, None)
    return jax.shard_map(local, mesh=mesh, in_specs=in_specs, out_specs=out_specs, check_vma=False)
```

```python
import jax
import jax.numpy as jnp
from jax import lax
from jax.experimental import pallas as pl
from jax.experimental.pallas import tpu as pltpu
from jax.sharding import PartitionSpec as P

epsilon = 1e-06
VMEM = pl.BlockSpec(memory_space=pltpu.VMEM)


def column(vector_ref):
    row = vector_ref[...].reshape(1, -1)
    count = row.shape[1]
    down = lax.broadcasted_iota(jnp.int32, (count, count), 0)
    across = lax.broadcasted_iota(jnp.int32, (count, count), 1)
    return jnp.sum(jnp.where(down == across, row, 0.0), axis=1, keepdims=True)


def norm_silu(values, gain):
    meansq = jnp.mean(values * values, axis=-2, keepdims=True)
    half = values * lax.rsqrt(meansq + epsilon) * (0.5 * gain)
    return half + half * jnp.tanh(half)


def activate(block, out, gain):
    for frame in range(block.shape[1]):
        for row in range(block.shape[2]):
            values = block[0, frame, row].astype(jnp.float32)
            out[frame, row] = norm_silu(values, gain).astype(jnp.bfloat16)


def restack(weights, offsets, out, lead=()):
    chans = weights.shape[0]
    blank = jnp.zeros((chans, chans), weights.dtype)
    for k in range(3):
        pieces = []
        for offset in offsets:
            if offset is None:
                pieces.append(blank)
            else:
                start = ((offset[0] * 3 + offset[1]) * 3 + k) * chans
                pieces.append(weights[:, start : start + chans])
        out[(*lead, slice(k * chans, (k + 1) * chans), slice(None))] = jnp.concatenate(pieces, axis=1)


def conv(weights, windows):
    columns = [jnp.concatenate(window, axis=0) for window in windows]
    stacked = jnp.dot(weights, jnp.concatenate(columns, axis=1), preferred_element_type=jnp.float32)
    chans, width = windows[0][0].shape
    lane = lax.broadcasted_iota(jnp.int32, (chans, width), 1)
    sums = []
    for index in range(len(windows)):
        part = stacked[:, index * width : (index + 1) * width]
        left = jnp.where(lane == 0, 0.0, pltpu.roll(part[:chans], 1, 1))
        right = jnp.where(lane == width - 1, 0.0, pltpu.roll(part[2 * chans :], width - 1, 1))
        sums.append(part[chans : 2 * chans] + left + right)
    return sums


def four_rows(top):
    return [(top, 0), (top, 1), (1 - top, 0), (1 - top, 1)]


def side_of_one():
    return 1 - lax.rem(lax.axis_index("rows"), 2)


def edge_kernel(valid):
    row_part = lax.axis_index("rows")
    one_below = lax.rem(row_part, 2) == 0
    has_above = row_part > 0
    has_below = row_part < lax.axis_size("rows") - 1
    later = lax.axis_index("tm") > 0
    has_one = (one_below & has_below) | (~one_below & has_above)
    has_two = (one_below & has_above) | (~one_below & has_below)
    for index, flag in enumerate((has_one, has_two, later, later & has_one, later & has_two)):
        valid[index] = jnp.broadcast_to(jnp.where(flag, 1.0, 0.0), valid.shape[1:])


def weights_kernel(kernel_first, kernel_second, first, double, single, second, second_12, second_2):
    weights = kernel_first[...]
    restack(weights, [(i, j) if j < 3 else None for i in range(3) for j in range(4)], first)
    restack(weights, [(i, j) for i in range(3) for j in (0, 1)], double, (0,))
    restack(weights, [(i, j) for i in range(3) for j in (1, 2)], double, (1,))
    restack(weights, [(i, 0) for i in range(3)], single, (0,))
    restack(weights, [(i, 2) for i in range(3)], single, (1,))
    weights = kernel_second[...]
    restack(weights, [(i, j) for i in range(3) for j in range(3)], second)
    restack(weights, [(i, j) for i in (1, 2) for j in range(3)], second_12)
    restack(weights, [(2, j) for j in range(3)], second_2)


def own_kernel(video, gamma_first, bias_first, gamma_second, bias_second, own, columns):
    for index, vector in enumerate((gamma_first, bias_first, gamma_second, bias_second)):
        columns[index] = jnp.broadcast_to(column(vector), columns.shape[1:])
    activate(video, own, columns[0])


def present_frames(cells, side, exists, first, columns, partial, late):
    bias, gain = columns[1], columns[2]
    depth = first.shape[1] // 3
    frames = cells.shape[1]
    rows = four_rows(side)
    for frame in range(frames):
        count = min(frame + 1, 3)
        windows = []
        for row in range(2):
            chosen = rows[row : row + 3] + rows[row + 1 : row + 2]
            windows.append([cells[a, f, r] for f in range(frame + 1 - count, frame + 1) for a, r in chosen])
        sums = conv(first[:, (3 - count) * depth :], windows)
        for row in range(2):
            hidden = sums[row] + bias
            if frame < 2:
                partial[frame, row] = hidden
            else:
                mask = jnp.where(side == row, exists, 1.0)
                late[frame - 2, row] = (norm_silu(hidden, gain) * mask).astype(jnp.bfloat16)


def earlier_sums(double, single, pair, row):
    frames = pair.shape[0]
    both, alone = [None] * 4, [None] * 4
    for group in ((0, 1), (2,), (3,)):
        count = min(3, 4 - group[0])
        span = {frame: range(frames - 4 + frame, frames - 4 + frame + count) for frame in group}
        depth = 2 * count * pair.shape[2]
        sums = conv(double[:, :depth], [[pair[f, r] for f in span[frame] for r in range(2)] for frame in group])
        for frame, value in zip(group, sums):
            both[frame] = value
        sums = conv(single[:, : depth // 2], [[pair[f, row] for f in span[frame]] for frame in group])
        for frame, value in zip(group, sums):
            alone[frame] = value
    return both, alone


def earlier_rest(double, single, inner, side, partial, bias, rest):
    both, alone = earlier_sums(double.at[1 - side], single.at[1 - side], inner, side)
    for frame in range(4):
        for index, (value, row) in enumerate(((alone[frame], side), (both[frame], 1 - side))):
            rest[frame, index] = value + (bias if frame < 2 else partial[frame - 2, row])


def earlier_frames(double, single, near, side, rest, exists, later, gain, early, lead=()):
    both, alone = earlier_sums(double.at[side], single.at[side], near, 1 - side)
    for frame in range(4):
        for index, (value, row) in enumerate(((both[frame], side), (alone[frame], 1 - side))):
            value = norm_silu(value + rest[frame, index], gain)
            if index == 0:
                value = value * exists
            if frame < 2:
                value = value * later
            early[(*lead, frame, row)] = value.astype(jnp.bfloat16)


def one_kernel(valid, one, own, first, columns, partial, late, cells):
    activate(one, cells.at[0], columns[0] * valid[0, 0:1])
    cells[1] = own[...]
    present_frames(cells, side_of_one(), valid[0, 0:1], first, columns, partial, late)


def two_kernel(
    valid, two, prior, own, first, double, single, second_12, second_2, columns, partial_one, late_one,
    rest_one, rest_two, late_sums, cells, inner, partial, late,
):
    side = side_of_one()
    activate(two, cells.at[0], columns[0] * valid[1, 0:1])
    cells[1] = own[...]
    activate(prior, inner, columns[0] * valid[2, 0:1])
    late[0] = late_one[...]
    present_frames(cells, 1 - side, valid[1, 0:1], first, columns, partial, late.at[1])
    earlier_rest(double, single, inner, side, partial_one, columns[1], rest_one)
    earlier_rest(double, single, inner, 1 - side, partial, columns[1], rest_two)
    rows = four_rows(side)
    for frame, weights in ((0, second_2), (1, second_12)):
        windows = [[late[a, f, r] for f in range(frame + 1) for a, r in rows[row : row + 3]] for row in range(2)]
        for row, value in enumerate(conv(weights[...], windows)):
            late_sums[frame, row] = value + columns[3]


def prior_kernel(valid, prior_one, double, single, columns, rest, early, near):
    activate(prior_one, near, columns[0] * valid[3, 0:1])
    earlier_frames(
        double, single, near, side_of_one(), rest, valid[0, 0:1], valid[2, 0:1], columns[2], early
    )


def last_kernel(
    valid, video, prior_two, double, single, second, columns, rest, early_one, late_sums,
    encoded, near, early,
):
    side = side_of_one()
    activate(prior_two, near, columns[0] * valid[4, 0:1])
    early[0] = early_one[...]
    earlier_frames(
        double, single, near, 1 - side, rest, valid[1, 0:1], valid[2, 0:1], columns[2], early, (1,)
    )
    rows = four_rows(side)
    for frame in range(4):
        count = min(3, 4 - frame)
        windows = [
            [early[a, f, r] for f in range(frame, frame + count) for a, r in rows[row : row + 3]]
            for row in range(2)
        ]
        sums = conv(second[:, : 3 * count * near.shape[2]], windows)
        for row in range(2):
            rest_of_sum = columns[3] if frame < 2 else late_sums[frame - 2, row]
            value = video[0, frame, row].astype(jnp.float32) + (sums[row] + rest_of_sum)
            encoded[0, frame, row] = value.astype(jnp.bfloat16)


def routed(block, goal):
    row_parts, frame_parts = lax.axis_size("rows"), lax.axis_size("tm")
    route = []
    for row in range(row_parts):
        for part in range(frame_parts):
            row_to, part_to = goal(row, part, row_parts, frame_parts)
            route.append((row * frame_parts + part, row_to * frame_parts + part_to))
    return lax.ppermute(block, ("rows", "tm"), route)


def later(row, part, row_parts, frame_parts):
    return row, (part + 1) % frame_parts


def paired(row, part, partner, row_parts, frame_parts):
    if 0 <= partner < row_parts:
        return partner, part
    return row, min(part ^ 1, frame_parts - 1)


def even_pair(row, part, row_parts, frame_parts):
    return paired(row, part, row + 1 - 2 * (row % 2), row_parts, frame_parts)


def odd_pair(row, part, row_parts, frame_parts):
    return paired(row, part, row - 1 + 2 * (row % 2), row_parts, frame_parts)


def exchange(video):
    prior = routed(video, later)
    two = routed(video, odd_pair)
    one = routed(video, even_pair)
    prior_two = routed(prior, odd_pair)
    prior_one = routed(prior, even_pair)
    return one, two, prior, prior_one, prior_two


def local(video, gamma_first, kernel_first, bias_first, gamma_second, kernel_second, bias_second):
    _, frames, rows, chans, width = video.shape
    assert frames == 4 and rows == 2
    one, two, prior, prior_one, prior_two = exchange(video)
    bf16, f32 = jnp.bfloat16, jnp.float32
    shape = jax.ShapeDtypeStruct
    params = pltpu.CompilerParams(vmem_limit_bytes=24 * 2**20)

    def run(kernel, out_shape, operands, scratch=(), millions=1000):
        single_out = not isinstance(out_shape, tuple)
        return pl.pallas_call(
            kernel,
            out_shape=out_shape,
            in_specs=[VMEM] * len(operands),
            out_specs=VMEM if single_out else [VMEM] * len(out_shape),
            scratch_shapes=[pltpu.VMEM(*one_scratch) for one_scratch in scratch],
            compiler_params=params,
            cost_estimate=pl.CostEstimate(flops=millions * 10**6, bytes_accessed=10**6, transcendentals=10**5),
        )(*operands)

    def stacked(*lead_and_taps):
        *lead, taps = lead_and_taps
        return shape((*lead, 3 * chans, taps * chans), bf16)

    block = (frames, rows, chans, width)
    cells = ((2, *block), bf16)
    pair = shape((2, 2, chans, width), f32)
    late = shape((2, 2, chans, width), bf16)
    rest = shape((4, 2, chans, width), f32)
    early = shape((4, 2, chans, width), bf16)
    valid = run(edge_kernel, shape((5, 8, width), f32), (), millions=2000)
    first, double, single, second, second_12, second_2 = run(
        weights_kernel,
        (stacked(12), stacked(2, 6), stacked(2, 3), stacked(9), stacked(6), stacked(3)),
        (kernel_first, kernel_second),
        millions=2000,
    )
    own, columns = run(
        own_kernel,
        (shape(block, bf16), shape((4, chans, width), f32)),
        (video, gamma_first, bias_first, gamma_second, bias_second),
        millions=1000,
    )
    partial_one, late_one = run(one_kernel, (pair, late), (valid, one, own, first, columns), (cells,), 10)
    rest_one, rest_two, late_sums = run(
        two_kernel,
        (rest, rest, pair),
        (valid, two, prior, own, first, double, single, second_12, second_2, columns, partial_one, late_one),
        (cells, (block, bf16), (pair.shape, f32), ((2, *late.shape), bf16)),
        10,
    )
    early_one = run(prior_kernel, early, (valid, prior_one, double, single, columns, rest_one), ((block, bf16),), 1000)
    return run(
        last_kernel,
        shape(video.shape, bf16),
        (valid, video, prior_two, double, single, second, columns, rest_two, early_one, late_sums),
        ((block, bf16), ((2, *early.shape), bf16)),
        1000,
    )


def solution(mesh):
    in_specs = (P("groups", "tm", "rows", None, None), P(), P(), P(), P(), P(), P())
    out_specs = P("groups", "tm", "rows", None, None)
    return jax.shard_map(local, mesh=mesh, in_specs=in_specs, out_specs=out_specs, check_vma=False)
```

```python
import itertools

import jax
import jax.numpy as jnp
from jax import lax
from jax.experimental import pallas as pl
from jax.experimental.pallas import tpu as pltpu
from jax.sharding import PartitionSpec as P

epsilon = 1e-06
VMEM = pl.BlockSpec(memory_space=pltpu.VMEM)


def column(vector_ref):
    row = vector_ref[...].reshape(1, -1)
    count = row.shape[1]
    down = lax.broadcasted_iota(jnp.int32, (count, count), 0)
    across = lax.broadcasted_iota(jnp.int32, (count, count), 1)
    return jnp.sum(jnp.where(down == across, row, 0.0), axis=1, keepdims=True)


def norm_silu(values, gain):
    meansq = jnp.mean(values * values, axis=-2, keepdims=True)
    half = values * lax.rsqrt(meansq + epsilon) * (0.5 * gain)
    return half + half * jnp.tanh(half)


def activate(block, out, gain):
    for frame in range(block.shape[1]):
        for row in range(block.shape[2]):
            values = block[0, frame, row].astype(jnp.float32)
            out[frame, row] = norm_silu(values, gain).astype(jnp.bfloat16)


def restack(weights, offsets, out, lead=()):
    chans = weights.shape[0]
    blank = jnp.zeros((chans, chans), weights.dtype)
    for k in range(3):
        pieces = []
        for offset in offsets:
            if offset is None:
                pieces.append(blank)
            else:
                start = ((offset[0] * 3 + offset[1]) * 3 + k) * chans
                pieces.append(weights[:, start : start + chans])
        out[(*lead, slice(k * chans, (k + 1) * chans), slice(None))] = jnp.concatenate(pieces, axis=1)


def conv(weights, windows):
    columns = [jnp.concatenate(window, axis=0) for window in windows]
    stacked = jnp.dot(weights, jnp.concatenate(columns, axis=1), preferred_element_type=jnp.float32)
    chans, width = windows[0][0].shape
    lane = lax.broadcasted_iota(jnp.int32, (chans, width), 1)
    sums = []
    for index in range(len(windows)):
        part = stacked[:, index * width : (index + 1) * width]
        left = jnp.where(lane == 0, 0.0, pltpu.roll(part[:chans], 1, 1))
        right = jnp.where(lane == width - 1, 0.0, pltpu.roll(part[2 * chans :], width - 1, 1))
        sums.append(part[chans : 2 * chans] + left + right)
    return sums


def four_rows(top):
    return [(top, 0), (top, 1), (1 - top, 0), (1 - top, 1)]


def side_of_one():
    return 1 - lax.rem(lax.axis_index("rows"), 2)


def edge_kernel(valid):
    row_part = lax.axis_index("rows")
    one_below = lax.rem(row_part, 2) == 0
    has_above = row_part > 0
    has_below = row_part < lax.axis_size("rows") - 1
    later = lax.axis_index("tm") > 0
    has_one = (one_below & has_below) | (~one_below & has_above)
    has_two = (one_below & has_above) | (~one_below & has_below)
    for index, flag in enumerate((has_one, has_two, later, later & has_one, later & has_two)):
        valid[index] = jnp.broadcast_to(jnp.where(flag, 1.0, 0.0), valid.shape[1:])


def weights_kernel(kernel_first, kernel_second, first, double, single, second, second_12, second_2):
    weights = kernel_first[...]
    restack(weights, [(i, j) if j < 3 else None for i in range(3) for j in range(4)], first)
    restack(weights, [(i, j) for i in range(3) for j in (0, 1)], double, (0,))
    restack(weights, [(i, j) for i in range(3) for j in (1, 2)], double, (1,))
    restack(weights, [(i, 0) for i in range(3)], single, (0,))
    restack(weights, [(i, 2) for i in range(3)], single, (1,))
    weights = kernel_second[...]
    restack(weights, [(i, j) for i in range(3) for j in range(3)], second)
    restack(weights, [(i, j) for i in (1, 2) for j in range(3)], second_12)
    restack(weights, [(2, j) for j in range(3)], second_2)


def own_kernel(video, gamma_first, bias_first, gamma_second, bias_second, own, columns):
    for index, vector in enumerate((gamma_first, bias_first, gamma_second, bias_second)):
        columns[index] = jnp.broadcast_to(column(vector), columns.shape[1:])
    activate(video, own, columns[0])


def present_frames(cells, side, exists, first, columns, partial, late):
    bias, gain = columns[1], columns[2]
    depth = first.shape[1] // 3
    frames = cells.shape[1]
    rows = four_rows(side)
    for frame in range(frames):
        count = min(frame + 1, 3)
        windows = []
        for row in range(2):
            chosen = rows[row : row + 3] + rows[row + 1 : row + 2]
            windows.append([cells[a, f, r] for f in range(frame + 1 - count, frame + 1) for a, r in chosen])
        sums = conv(first[:, (3 - count) * depth :], windows)
        for row in range(2):
            hidden = sums[row] + bias
            if frame < 2:
                partial[frame, row] = hidden
            else:
                mask = jnp.where(side == row, exists, 1.0)
                late[frame - 2, row] = (norm_silu(hidden, gain) * mask).astype(jnp.bfloat16)


def earlier_sums(double, single, pair, row):
    frames = pair.shape[0]
    both, alone = [None] * 4, [None] * 4
    for group in ((0, 1), (2,), (3,)):
        count = min(3, 4 - group[0])
        span = {frame: range(frames - 4 + frame, frames - 4 + frame + count) for frame in group}
        depth = 2 * count * pair.shape[2]
        sums = conv(double[:, :depth], [[pair[f, r] for f in span[frame] for r in range(2)] for frame in group])
        for frame, value in zip(group, sums):
            both[frame] = value
        sums = conv(single[:, : depth // 2], [[pair[f, row] for f in span[frame]] for frame in group])
        for frame, value in zip(group, sums):
            alone[frame] = value
    return both, alone


def earlier_rest(double, single, inner, side, partial, bias, rest):
    both, alone = earlier_sums(double.at[1 - side], single.at[1 - side], inner, side)
    for frame in range(4):
        for index, (value, row) in enumerate(((alone[frame], side), (both[frame], 1 - side))):
            rest[frame, index] = value + (bias if frame < 2 else partial[frame - 2, row])


def earlier_frames(double, single, near, side, rest, exists, later, gain, early, lead=()):
    both, alone = earlier_sums(double.at[side], single.at[side], near, 1 - side)
    for frame in range(4):
        for index, (value, row) in enumerate(((both[frame], side), (alone[frame], 1 - side))):
            value = norm_silu(value + rest[frame, index], gain)
            if index == 0:
                value = value * exists
            if frame < 2:
                value = value * later
            early[(*lead, frame, row)] = value.astype(jnp.bfloat16)


def one_kernel(valid, one, own, first, columns, partial, late, cells):
    activate(one, cells.at[0], columns[0] * valid[0, 0:1])
    cells[1] = own[...]
    present_frames(cells, side_of_one(), valid[0, 0:1], first, columns, partial, late)


def two_kernel(
    valid, two, prior, own, first, double, single, second_12, second_2, columns, partial_one, late_one,
    rest_one, rest_two, late_sums, cells, inner, partial, late,
):
    side = side_of_one()
    activate(two, cells.at[0], columns[0] * valid[1, 0:1])
    cells[1] = own[...]
    activate(prior, inner, columns[0] * valid[2, 0:1])
    late[0] = late_one[...]
    present_frames(cells, 1 - side, valid[1, 0:1], first, columns, partial, late.at[1])
    earlier_rest(double, single, inner, side, partial_one, columns[1], rest_one)
    earlier_rest(double, single, inner, 1 - side, partial, columns[1], rest_two)
    rows = four_rows(side)
    for frame, weights in ((0, second_2), (1, second_12)):
        windows = [[late[a, f, r] for f in range(frame + 1) for a, r in rows[row : row + 3]] for row in range(2)]
        for row, value in enumerate(conv(weights[...], windows)):
            late_sums[frame, row] = value + columns[3]


def prior_kernel(valid, prior_one, double, single, columns, rest, early, near):
    activate(prior_one, near, columns[0] * valid[3, 0:1])
    earlier_frames(
        double, single, near, side_of_one(), rest, valid[0, 0:1], valid[2, 0:1], columns[2], early
    )


def last_kernel(
    valid, video, prior_two, double, single, second, columns, rest, early_one, late_sums,
    encoded, near, early,
):
    side = side_of_one()
    activate(prior_two, near, columns[0] * valid[4, 0:1])
    early[0] = early_one[...]
    earlier_frames(
        double, single, near, 1 - side, rest, valid[1, 0:1], valid[2, 0:1], columns[2], early, (1,)
    )
    rows = four_rows(side)
    for frame in range(4):
        count = min(3, 4 - frame)
        windows = [
            [early[a, f, r] for f in range(frame, frame + count) for a, r in rows[row : row + 3]]
            for row in range(2)
        ]
        sums = conv(second[:, : 3 * count * near.shape[2]], windows)
        for row in range(2):
            rest_of_sum = columns[3] if frame < 2 else late_sums[frame - 2, row]
            value = video[0, frame, row].astype(jnp.float32) + (sums[row] + rest_of_sum)
            encoded[0, frame, row] = value.astype(jnp.bfloat16)


def routed(block, goal):
    sizes = [lax.axis_size(axis) for axis in ("groups", "rows", "tm")]
    places = list(itertools.product(*map(range, sizes)))
    route = [(index, places.index(goal(place, sizes))) for index, place in enumerate(places)]
    return lax.ppermute(block, ("groups", "rows", "tm"), route)


def later(place, sizes):
    group, row, part = place
    return group, row, (part + 1) % sizes[2]


def paired(place, sizes, partner):
    group, row, part = place
    if 0 <= partner < sizes[1]:
        return group, partner, part
    return group, row, min(part ^ 1, sizes[2] - 1)


def even_pair(place, sizes):
    return paired(place, sizes, place[1] + 1 - 2 * (place[1] % 2))


def odd_pair(place, sizes):
    return paired(place, sizes, place[1] - 1 + 2 * (place[1] % 2))


def if_earlier(pair):
    def goal(place, sizes):
        group, row, part = place
        if part == 0 and pair(place, sizes)[1] != row and group ^ 1 < sizes[0]:
            return group ^ 1, row, part
        return pair(place, sizes)

    return goal


def exchange(video):
    prior = routed(video, later)
    two = routed(video, odd_pair)
    one = routed(video, even_pair)
    prior_two = routed(prior, if_earlier(odd_pair))
    prior_one = routed(prior, if_earlier(even_pair))
    return one, two, prior, prior_one, prior_two


def local(video, gamma_first, kernel_first, bias_first, gamma_second, kernel_second, bias_second):
    _, frames, rows, chans, width = video.shape
    assert frames == 4 and rows == 2
    one, two, prior, prior_one, prior_two = exchange(video)
    bf16, f32 = jnp.bfloat16, jnp.float32
    shape = jax.ShapeDtypeStruct
    params = pltpu.CompilerParams(vmem_limit_bytes=24 * 2**20)

    def run(kernel, out_shape, operands, scratch=(), millions=1000):
        single_out = not isinstance(out_shape, tuple)
        return pl.pallas_call(
            kernel,
            out_shape=out_shape,
            in_specs=[VMEM] * len(operands),
            out_specs=VMEM if single_out else [VMEM] * len(out_shape),
            scratch_shapes=[pltpu.VMEM(*one_scratch) for one_scratch in scratch],
            compiler_params=params,
            cost_estimate=pl.CostEstimate(flops=millions * 10**6, bytes_accessed=10**6, transcendentals=10**5),
        )(*operands)

    def stacked(*lead_and_taps):
        *lead, taps = lead_and_taps
        return shape((*lead, 3 * chans, taps * chans), bf16)

    block = (frames, rows, chans, width)
    cells = ((2, *block), bf16)
    pair = shape((2, 2, chans, width), f32)
    late = shape((2, 2, chans, width), bf16)
    rest = shape((4, 2, chans, width), f32)
    early = shape((4, 2, chans, width), bf16)
    valid = run(edge_kernel, shape((5, 8, width), f32), (), millions=2000)
    first, double, single, second, second_12, second_2 = run(
        weights_kernel,
        (stacked(12), stacked(2, 6), stacked(2, 3), stacked(9), stacked(6), stacked(3)),
        (kernel_first, kernel_second),
        millions=2000,
    )
    own, columns = run(
        own_kernel,
        (shape(block, bf16), shape((4, chans, width), f32)),
        (video, gamma_first, bias_first, gamma_second, bias_second),
        millions=1000,
    )
    partial_one, late_one = run(one_kernel, (pair, late), (valid, one, own, first, columns), (cells,), 10)
    rest_one, rest_two, late_sums = run(
        two_kernel,
        (rest, rest, pair),
        (valid, two, prior, own, first, double, single, second_12, second_2, columns, partial_one, late_one),
        (cells, (block, bf16), (pair.shape, f32), ((2, *late.shape), bf16)),
        10,
    )
    early_one = run(prior_kernel, early, (valid, prior_one, double, single, columns, rest_one), ((block, bf16),), 1000)
    return run(
        last_kernel,
        shape(video.shape, bf16),
        (valid, video, prior_two, double, single, second, columns, rest_two, early_one, late_sums),
        ((block, bf16), ((2, *early.shape), bf16)),
        1000,
    )


def solution(mesh):
    in_specs = (P("groups", "tm", "rows", None, None), P(), P(), P(), P(), P(), P())
    out_specs = P("groups", "tm", "rows", None, None)
    return jax.shard_map(local, mesh=mesh, in_specs=in_specs, out_specs=out_specs, check_vma=False)
```

```python
import itertools

import jax
import jax.numpy as jnp
from jax import lax
from jax.experimental import pallas as pl
from jax.experimental.pallas import tpu as pltpu
from jax.sharding import PartitionSpec as P

epsilon = 1e-06
VMEM = pl.BlockSpec(memory_space=pltpu.VMEM)


def column(vector_ref):
    row = vector_ref[...].reshape(1, -1)
    count = row.shape[1]
    down = lax.broadcasted_iota(jnp.int32, (count, count), 0)
    across = lax.broadcasted_iota(jnp.int32, (count, count), 1)
    return jnp.sum(jnp.where(down == across, row, 0.0), axis=1, keepdims=True)


def norm_silu(values, gain):
    meansq = jnp.mean(values * values, axis=-2, keepdims=True)
    half = values * lax.rsqrt(meansq + epsilon) * (0.5 * gain)
    return half + half * jnp.tanh(half)


def activate(block, out, gain):
    for frame in range(block.shape[1]):
        for row in range(block.shape[2]):
            values = block[0, frame, row].astype(jnp.float32)
            out[frame, row] = norm_silu(values, gain).astype(jnp.bfloat16)


def restack(weights, offsets, out, lead=()):
    chans = weights.shape[0]
    blank = jnp.zeros((chans, chans), weights.dtype)
    for k in range(3):
        pieces = []
        for offset in offsets:
            if offset is None:
                pieces.append(blank)
            else:
                start = ((offset[0] * 3 + offset[1]) * 3 + k) * chans
                pieces.append(weights[:, start : start + chans])
        out[(*lead, slice(k * chans, (k + 1) * chans), slice(None))] = jnp.concatenate(pieces, axis=1)


def conv(weights, windows):
    columns = [jnp.concatenate(window, axis=0) for window in windows]
    stacked = jnp.dot(weights, jnp.concatenate(columns, axis=1), preferred_element_type=jnp.float32)
    chans, width = windows[0][0].shape
    lane = lax.broadcasted_iota(jnp.int32, (chans, width), 1)
    sums = []
    for index in range(len(windows)):
        part = stacked[:, index * width : (index + 1) * width]
        left = jnp.where(lane == 0, 0.0, pltpu.roll(part[:chans], 1, 1))
        right = jnp.where(lane == width - 1, 0.0, pltpu.roll(part[2 * chans :], width - 1, 1))
        sums.append(part[chans : 2 * chans] + left + right)
    return sums


def four_rows(top):
    return [(top, 0), (top, 1), (1 - top, 0), (1 - top, 1)]


def side_of_one():
    return 1 - lax.rem(lax.axis_index("rows"), 2)


def edge_kernel(valid):
    row_part = lax.axis_index("rows")
    one_below = lax.rem(row_part, 2) == 0
    has_above = row_part > 0
    has_below = row_part < lax.axis_size("rows") - 1
    later = lax.axis_index("tm") > 0
    has_one = (one_below & has_below) | (~one_below & has_above)
    has_two = (one_below & has_above) | (~one_below & has_below)
    for index, flag in enumerate((has_one, has_two, later)):
        valid[index] = jnp.broadcast_to(jnp.where(flag, 1.0, 0.0), valid.shape[1:])


def weights_kernel(kernel_first, kernel_second, first, double, single, second, second_12, second_2):
    weights = kernel_first[...]
    restack(weights, [(i, j) if j < 3 else None for i in range(3) for j in range(4)], first)
    restack(weights, [(i, j) for i in range(3) for j in (0, 1)], double, (0,))
    restack(weights, [(i, j) for i in range(3) for j in (1, 2)], double, (1,))
    restack(weights, [(i, 0) for i in range(3)], single, (0,))
    restack(weights, [(i, 2) for i in range(3)], single, (1,))
    weights = kernel_second[...]
    restack(weights, [(i, j) for i in range(3) for j in range(3)], second)
    restack(weights, [(i, j) for i in (1, 2) for j in range(3)], second_12)
    restack(weights, [(2, j) for j in range(3)], second_2)


def own_kernel(video, gamma_first, bias_first, gamma_second, bias_second, own, columns):
    for index, vector in enumerate((gamma_first, bias_first, gamma_second, bias_second)):
        columns[index] = jnp.broadcast_to(column(vector), columns.shape[1:])
    activate(video, own, columns[0])


def present_frames(cells, side, exists, first, columns, partial, late):
    bias, gain = columns[1], columns[2]
    depth = first.shape[1] // 3
    frames = cells.shape[1]
    rows = four_rows(side)
    for frame in range(frames):
        count = min(frame + 1, 3)
        windows = []
        for row in range(2):
            chosen = rows[row : row + 3] + rows[row + 1 : row + 2]
            windows.append([cells[a, f, r] for f in range(frame + 1 - count, frame + 1) for a, r in chosen])
        sums = conv(first[:, (3 - count) * depth :], windows)
        for row in range(2):
            hidden = sums[row] + bias
            if frame < 2:
                partial[frame, row] = hidden
            else:
                mask = jnp.where(side == row, exists, 1.0)
                late[frame - 2, row] = (norm_silu(hidden, gain) * mask).astype(jnp.bfloat16)


def earlier_sums(double, single, pair, row):
    frames, _, chans, width = pair.shape
    blank = jnp.zeros((chans, width), pair.dtype)
    both, alone = [None] * 4, [None] * 4
    for group, count in (((0, 1), 3), ((2, 3), 2)):
        span = {frame: range(frames - 4 + frame, frames - 4 + frame + count) for frame in group}
        depth = 2 * count * chans
        read = lambda f, r: pair[f, r] if f < frames else blank
        sums = conv(double[:, :depth], [[read(f, r) for f in span[frame] for r in range(2)] for frame in group])
        for frame, value in zip(group, sums):
            both[frame] = value
        sums = conv(single[:, : depth // 2], [[read(f, row) for f in span[frame]] for frame in group])
        for frame, value in zip(group, sums):
            alone[frame] = value
    return both, alone


def earlier_rest(double, single, inner, side, partial, bias, rest):
    both, alone = earlier_sums(double.at[1 - side], single.at[1 - side], inner, side)
    for frame in range(4):
        for index, (value, row) in enumerate(((alone[frame], side), (both[frame], 1 - side))):
            rest[frame, index] = value + (bias if frame < 2 else partial[frame - 2, row])


def earlier_frames(double, single, near, side, rest, exists, later, gain, early, lead=()):
    both, alone = earlier_sums(double.at[side], single.at[side], near, 1 - side)
    for frame in range(4):
        for index, (value, row) in enumerate(((both[frame], side), (alone[frame], 1 - side))):
            value = norm_silu(value * exists + rest[frame, index], gain)
            if index == 0:
                value = value * exists
            if frame < 2:
                value = value * later
            early[(*lead, frame, row)] = value.astype(jnp.bfloat16)


def one_kernel(valid, one, own, first, columns, partial, late, cells):
    activate(one, cells.at[0], columns[0] * valid[0, 0:1])
    cells[1] = own[...]
    present_frames(cells, side_of_one(), valid[0, 0:1], first, columns, partial, late)


def two_kernel(
    valid, two, inner, own, first, double, single, second_12, second_2, columns, partial_one, late_one,
    rest_one, rest_two, late_sums, cells, partial, late,
):
    side = side_of_one()
    activate(two, cells.at[0], columns[0] * valid[1, 0:1])
    cells[1] = own[...]
    late[0] = late_one[...]
    present_frames(cells, 1 - side, valid[1, 0:1], first, columns, partial, late.at[1])
    earlier_rest(double, single, inner, side, partial_one, columns[1], rest_one)
    earlier_rest(double, single, inner, 1 - side, partial, columns[1], rest_two)
    rows = four_rows(side)
    for frame, weights in ((0, second_2), (1, second_12)):
        windows = [[late[a, f, r] for f in range(frame + 1) for a, r in rows[row : row + 3]] for row in range(2)]
        for row, value in enumerate(conv(weights[...], windows)):
            late_sums[frame, row] = value + columns[3]


def inner_kernel(valid, prior, columns, inner):
    activate(prior, inner, columns[0] * valid[2, 0:1])


def prior_kernel(valid, near, double, single, columns, rest, early):
    earlier_frames(
        double, single, near, side_of_one(), rest, valid[0, 0:1], valid[2, 0:1], columns[2], early
    )


def last_kernel(
    valid, video, near, double, single, second, columns, rest, early_one, late_sums,
    encoded, early,
):
    side = side_of_one()
    early[0] = early_one[...]
    earlier_frames(
        double, single, near, 1 - side, rest, valid[1, 0:1], valid[2, 0:1], columns[2], early, (1,)
    )
    rows = four_rows(side)
    for frame in range(4):
        count = min(3, 4 - frame)
        windows = [
            [early[a, f, r] for f in range(frame, frame + count) for a, r in rows[row : row + 3]]
            for row in range(2)
        ]
        sums = conv(second[:, : 3 * count * near.shape[2]], windows)
        for row in range(2):
            rest_of_sum = columns[3] if frame < 2 else late_sums[frame - 2, row]
            value = video[0, frame, row].astype(jnp.float32) + (sums[row] + rest_of_sum)
            encoded[0, frame, row] = value.astype(jnp.bfloat16)


def routed(block, goal):
    sizes = [lax.axis_size(axis) for axis in ("groups", "rows", "tm")]
    places = list(itertools.product(*map(range, sizes)))
    route = [(index, places.index(goal(place, sizes))) for index, place in enumerate(places)]
    return lax.ppermute(block, ("groups", "rows", "tm"), route)


def later(place, sizes):
    group, row, part = place
    return group, row, (part + 1) % sizes[2]


def paired(place, sizes, partner):
    group, row, part = place
    if 0 <= partner < sizes[1]:
        return group, partner, part
    return group, row, min(part ^ 1, sizes[2] - 1)


def even_pair(place, sizes):
    return paired(place, sizes, place[1] + 1 - 2 * (place[1] % 2))


def odd_pair(place, sizes):
    return paired(place, sizes, place[1] - 1 + 2 * (place[1] % 2))


def if_earlier(pair):
    def goal(place, sizes):
        group, row, part = place
        if part == 0 and pair(place, sizes)[1] != row and group ^ 1 < sizes[0]:
            return group ^ 1, row, part
        return pair(place, sizes)

    return goal


def local(video, gamma_first, kernel_first, bias_first, gamma_second, kernel_second, bias_second):
    _, frames, rows, chans, width = video.shape
    assert frames == 4 and rows == 2
    prior = routed(video, later)
    two = routed(video, odd_pair)
    one = routed(video, even_pair)
    bf16, f32 = jnp.bfloat16, jnp.float32
    shape = jax.ShapeDtypeStruct
    params = pltpu.CompilerParams(vmem_limit_bytes=24 * 2**20)

    def run(kernel, out_shape, operands, scratch=(), millions=1000):
        single_out = not isinstance(out_shape, tuple)
        return pl.pallas_call(
            kernel,
            out_shape=out_shape,
            in_specs=[VMEM] * len(operands),
            out_specs=VMEM if single_out else [VMEM] * len(out_shape),
            scratch_shapes=[pltpu.VMEM(*one_scratch) for one_scratch in scratch],
            compiler_params=params,
            cost_estimate=pl.CostEstimate(flops=millions * 10**6, bytes_accessed=10**6, transcendentals=10**5),
        )(*operands)

    def stacked(*lead_and_taps):
        *lead, taps = lead_and_taps
        return shape((*lead, 3 * chans, taps * chans), bf16)

    block = (frames, rows, chans, width)
    cells = ((2, *block), bf16)
    pair = shape((2, 2, chans, width), f32)
    late = shape((2, 2, chans, width), bf16)
    rest = shape((4, 2, chans, width), f32)
    early = shape((4, 2, chans, width), bf16)
    valid = run(edge_kernel, shape((3, 8, width), f32), (), millions=2000)
    first, double, single, second, second_12, second_2 = run(
        weights_kernel,
        (stacked(12), stacked(2, 6), stacked(2, 3), stacked(9), stacked(6), stacked(3)),
        (kernel_first, kernel_second),
        millions=10,
    )
    own, columns = run(
        own_kernel,
        (shape(block, bf16), shape((4, chans, width), f32)),
        (video, gamma_first, bias_first, gamma_second, bias_second),
        millions=10,
    )
    inner = run(inner_kernel, shape(block, bf16), (valid, prior, columns), millions=10)
    prior_two = routed(inner, if_earlier(odd_pair))
    prior_one = routed(inner, if_earlier(even_pair))
    partial_one, late_one = run(one_kernel, (pair, late), (valid, one, own, first, columns), (cells,), 10)
    rest_one, rest_two, late_sums = run(
        two_kernel,
        (rest, rest, pair),
        (valid, two, inner, own, first, double, single, second_12, second_2, columns, partial_one, late_one),
        (cells, (pair.shape, f32), ((2, *late.shape), bf16)),
        10,
    )
    early_one = run(prior_kernel, early, (valid, prior_one, double, single, columns, rest_one), (), 1000)
    return run(
        last_kernel,
        shape(video.shape, bf16),
        (valid, video, prior_two, double, single, second, columns, rest_two, early_one, late_sums),
        (((2, *early.shape), bf16),),
        1000,
    )


def solution(mesh):
    in_specs = (P("groups", "tm", "rows", None, None), P(), P(), P(), P(), P(), P())
    out_specs = P("groups", "tm", "rows", None, None)
    return jax.shard_map(local, mesh=mesh, in_specs=in_specs, out_specs=out_specs, check_vma=False)
```

```python
import itertools

import jax
import jax.numpy as jnp
from jax import lax
from jax.experimental import pallas as pl
from jax.experimental.pallas import tpu as pltpu
from jax.sharding import PartitionSpec as P

epsilon = 1e-06
VMEM = pl.BlockSpec(memory_space=pltpu.VMEM)


def column(vector_ref):
    row = vector_ref[...].reshape(1, -1)
    count = row.shape[1]
    down = lax.broadcasted_iota(jnp.int32, (count, count), 0)
    across = lax.broadcasted_iota(jnp.int32, (count, count), 1)
    return jnp.sum(jnp.where(down == across, row, 0.0), axis=1, keepdims=True)


def norm_silu(values, gain):
    meansq = jnp.mean(values * values, axis=-2, keepdims=True)
    half = values * lax.rsqrt(meansq + epsilon) * (0.5 * gain)
    return half + half * jnp.tanh(half)


def activate(block, out, gain):
    for frame in range(block.shape[1]):
        for row in range(block.shape[2]):
            values = block[0, frame, row].astype(jnp.float32)
            out[frame, row] = norm_silu(values, gain).astype(jnp.bfloat16)


def restack(weights, offsets, out, lead=()):
    chans = weights.shape[0]
    blank = jnp.zeros((chans, chans), weights.dtype)
    for k in range(3):
        pieces = []
        for offset in offsets:
            if offset is None:
                pieces.append(blank)
            else:
                start = ((offset[0] * 3 + offset[1]) * 3 + k) * chans
                pieces.append(weights[:, start : start + chans])
        out[(*lead, slice(k * chans, (k + 1) * chans), slice(None))] = jnp.concatenate(pieces, axis=1)


def conv(weights, windows):
    columns = [jnp.concatenate(window, axis=0) for window in windows]
    stacked = jnp.dot(weights, jnp.concatenate(columns, axis=1), preferred_element_type=jnp.float32)
    chans, width = windows[0][0].shape
    lane = lax.broadcasted_iota(jnp.int32, (chans, width), 1)
    sums = []
    for index in range(len(windows)):
        part = stacked[:, index * width : (index + 1) * width]
        left = jnp.where(lane == 0, 0.0, pltpu.roll(part[:chans], 1, 1))
        right = jnp.where(lane == width - 1, 0.0, pltpu.roll(part[2 * chans :], width - 1, 1))
        sums.append(part[chans : 2 * chans] + left + right)
    return sums


def four_rows(top):
    return [(top, 0), (top, 1), (1 - top, 0), (1 - top, 1)]


def side_of_one():
    return 1 - lax.rem(lax.axis_index("rows"), 2)


def edge_kernel(valid):
    row_part = lax.axis_index("rows")
    one_below = lax.rem(row_part, 2) == 0
    has_above = row_part > 0
    has_below = row_part < lax.axis_size("rows") - 1
    later = lax.axis_index("tm") > 0
    has_one = (one_below & has_below) | (~one_below & has_above)
    has_two = (one_below & has_above) | (~one_below & has_below)
    for index, flag in enumerate((has_one, has_two, later)):
        valid[index] = jnp.broadcast_to(jnp.where(flag, 1.0, 0.0), valid.shape[1:])


def restack_sides(weights, double, single):
    restack(weights, [(i, j) for i in range(3) for j in (0, 1)], double, (0,))
    restack(weights, [(i, j) for i in range(3) for j in (1, 2)], double, (1,))
    restack(weights, [(i, 0) for i in range(3)], single, (0,))
    restack(weights, [(i, 2) for i in range(3)], single, (1,))


def own_kernel(
    valid, video, gamma_first, kernel_first, bias_first, gamma_second, kernel_second, bias_second,
    own, columns, first, double, single, second_double, second_single, second_12, second_2,
):
    for index, vector in enumerate((gamma_first, bias_first, gamma_second, bias_second)):
        columns[index] = jnp.broadcast_to(column(vector), columns.shape[1:])
    activate(video, own, columns[0])
    weights = kernel_first[...]
    restack(weights, [(i, j) if j < 3 else None for i in range(3) for j in range(4)], first)
    restack_sides(weights, double, single)
    weights = kernel_second[...]
    restack_sides(weights, second_double, second_single)
    restack(weights, [(i, j) for i in (1, 2) for j in range(3)], second_12)
    restack(weights, [(2, j) for j in range(3)], second_2)


def present_frames(cells, side, exists, first, columns, partial, late):
    bias, gain = columns[1], columns[2]
    depth = first.shape[1] // 3
    frames = cells.shape[1]
    rows = four_rows(side)
    for frame in range(frames):
        count = min(frame + 1, 3)
        windows = []
        for row in range(2):
            chosen = rows[row : row + 3] + rows[row + 1 : row + 2]
            windows.append([cells[a, f, r] for f in range(frame + 1 - count, frame + 1) for a, r in chosen])
        sums = conv(first[:, (3 - count) * depth :], windows)
        for row in range(2):
            hidden = sums[row] + bias
            if frame < 2:
                partial[frame, row] = hidden
            else:
                mask = jnp.where(side == row, exists, 1.0)
                late[frame - 2, row] = (norm_silu(hidden, gain) * mask).astype(jnp.bfloat16)


def earlier_sums(double, single, pair, row):
    frames, _, chans, width = pair.shape
    blank = jnp.zeros((chans, width), pair.dtype)
    both, alone = [None] * 4, [None] * 4
    for group, count in (((0, 1), 3), ((2, 3), 2)):
        span = {frame: range(frames - 4 + frame, frames - 4 + frame + count) for frame in group}
        depth = 2 * count * chans
        read = lambda f, r: pair[f, r] if f < frames else blank
        sums = conv(double[:, :depth], [[read(f, r) for f in span[frame] for r in range(2)] for frame in group])
        for frame, value in zip(group, sums):
            both[frame] = value
        sums = conv(single[:, : depth // 2], [[read(f, row) for f in span[frame]] for frame in group])
        for frame, value in zip(group, sums):
            alone[frame] = value
    return both, alone


def earlier_rest(double, single, inner, side, partial, bias, rest):
    both, alone = earlier_sums(double.at[1 - side], single.at[1 - side], inner, side)
    for frame in range(4):
        for index, (value, row) in enumerate(((alone[frame], side), (both[frame], 1 - side))):
            rest[frame, index] = value + (bias if frame < 2 else partial[frame - 2, row])


def earlier_frames(double, single, near, side, rest, exists, later, gain, early, lead=()):
    both, alone = earlier_sums(double.at[side], single.at[side], near, 1 - side)
    for frame in range(4):
        for index, (value, row) in enumerate(((both[frame], side), (alone[frame], 1 - side))):
            value = norm_silu(value * exists + rest[frame, index], gain)
            if index == 0:
                value = value * exists
            if frame < 2:
                value = value * later
            early[(*lead, frame, row)] = value.astype(jnp.bfloat16)


def one_kernel(valid, one, own, first, columns, partial, late, cells):
    activate(one, cells.at[0], columns[0] * valid[0, 0:1])
    cells[1] = own[...]
    present_frames(cells, side_of_one(), valid[0, 0:1], first, columns, partial, late)


def two_kernel(
    partial_one, late_one, valid, two, inner, own, first, double, single, second_12, second_2, columns,
    rest_one, rest_two, late_sums, cells, partial, late,
):
    side = side_of_one()
    activate(two, cells.at[0], columns[0] * valid[1, 0:1])
    cells[1] = own[...]
    late[0] = late_one[...]
    present_frames(cells, 1 - side, valid[1, 0:1], first, columns, partial, late.at[1])
    earlier_rest(double, single, inner, side, partial_one, columns[1], rest_one)
    earlier_rest(double, single, inner, 1 - side, partial, columns[1], rest_two)
    rows = four_rows(side)
    for frame, weights in ((0, second_2), (1, second_12)):
        windows = [[late[a, f, r] for f in range(frame + 1) for a, r in rows[row : row + 3]] for row in range(2)]
        for row, value in enumerate(conv(weights[...], windows)):
            late_sums[frame, row] = value + columns[3]


def inner_kernel(valid, prior, columns, inner):
    activate(prior, inner, columns[0] * valid[2, 0:1])


def prior_kernel(
    valid, video, near, double, single, second_double, second_single, columns, rest, late_sums, sums, early
):
    side = side_of_one()
    earlier_frames(double, single, near, side, rest, valid[0, 0:1], valid[2, 0:1], columns[2], early)
    both, alone = earlier_sums(second_double.at[side], second_single.at[side], early, 1 - side)
    for frame in range(4):
        for value, row in ((both[frame], side), (alone[frame], 1 - side)):
            rest_of_sum = columns[3] if frame < 2 else late_sums[frame - 2, row]
            sums[frame, row] = video[0, frame, row].astype(jnp.float32) + (value + rest_of_sum)


def last_kernel(valid, near, double, single, second_double, second_single, columns, rest, sums, encoded, early):
    side = 1 - side_of_one()
    earlier_frames(double, single, near, side, rest, valid[1, 0:1], valid[2, 0:1], columns[2], early)
    both, alone = earlier_sums(second_double.at[side], second_single.at[side], early, 1 - side)
    for frame in range(4):
        for value, row in ((both[frame], side), (alone[frame], 1 - side)):
            encoded[0, frame, row] = (sums[frame, row] + value).astype(jnp.bfloat16)


def routed(block, goal):
    sizes = [lax.axis_size(axis) for axis in ("groups", "rows", "tm")]
    places = list(itertools.product(*map(range, sizes)))
    route = [(index, places.index(goal(place, sizes))) for index, place in enumerate(places)]
    return lax.ppermute(block, ("groups", "rows", "tm"), route)


def later(place, sizes):
    group, row, part = place
    return group, row, (part + 1) % sizes[2]


def paired(place, sizes, partner):
    group, row, part = place
    if 0 <= partner < sizes[1]:
        return group, partner, part
    return group, row, min(part ^ 1, sizes[2] - 1)


def even_pair(place, sizes):
    return paired(place, sizes, place[1] + 1 - 2 * (place[1] % 2))


def odd_pair(place, sizes):
    return paired(place, sizes, place[1] - 1 + 2 * (place[1] % 2))


def if_earlier(pair):
    def goal(place, sizes):
        group, row, part = place
        if part == 0 and pair(place, sizes)[1] != row and group ^ 1 < sizes[0]:
            return group ^ 1, row, part
        return pair(place, sizes)

    return goal


def local(video, gamma_first, kernel_first, bias_first, gamma_second, kernel_second, bias_second):
    _, frames, rows, chans, width = video.shape
    assert frames == 4 and rows == 2
    prior = routed(video, later)
    two = routed(video, odd_pair)
    one = routed(video, even_pair)
    bf16, f32 = jnp.bfloat16, jnp.float32
    shape = jax.ShapeDtypeStruct
    params = pltpu.CompilerParams(vmem_limit_bytes=24 * 2**20)

    def run(kernel, out_shape, operands, scratch=(), millions=1000):
        single_out = not isinstance(out_shape, tuple)
        return pl.pallas_call(
            kernel,
            out_shape=out_shape,
            in_specs=[VMEM] * len(operands),
            out_specs=VMEM if single_out else [VMEM] * len(out_shape),
            scratch_shapes=[pltpu.VMEM(*one_scratch) for one_scratch in scratch],
            compiler_params=params,
            cost_estimate=pl.CostEstimate(flops=millions * 10**6, bytes_accessed=10**6, transcendentals=10**5),
        )(*operands)

    def stacked(*lead_and_taps):
        *lead, taps = lead_and_taps
        return shape((*lead, 3 * chans, taps * chans), bf16)

    block = (frames, rows, chans, width)
    cells = ((2, *block), bf16)
    pair = shape((2, 2, chans, width), f32)
    late = shape((2, 2, chans, width), bf16)
    rest = shape((4, 2, chans, width), f32)
    early = shape((4, 2, chans, width), bf16)
    valid = run(edge_kernel, shape((3, 8, width), f32), (), millions=2000)
    own, columns, first, double, single, second_double, second_single, second_12, second_2 = run(
        own_kernel,
        (
            shape(block, bf16),
            shape((4, chans, width), f32),
            *(stacked(12), stacked(2, 6), stacked(2, 3), stacked(2, 6), stacked(2, 3), stacked(6), stacked(3)),
        ),
        (valid, video, gamma_first, kernel_first, bias_first, gamma_second, kernel_second, bias_second),
        millions=10,
    )
    inner = run(inner_kernel, shape(block, bf16), (valid, prior, columns), millions=10)
    prior_two = routed(inner, if_earlier(odd_pair))
    prior_one = routed(inner, if_earlier(even_pair))
    partial_one, late_one = run(one_kernel, (pair, late), (valid, one, own, first, columns), (cells,), 10)
    rest_one, rest_two, late_sums = run(
        two_kernel,
        (rest, rest, pair),
        (partial_one, late_one, valid, two, inner, own, first, double, single, second_12, second_2, columns),
        (cells, (pair.shape, f32), ((2, *late.shape), bf16)),
        10,
    )
    sums = run(
        prior_kernel,
        rest,
        (valid, video, prior_one, double, single, second_double, second_single, columns, rest_one, late_sums),
        ((early.shape, bf16),),
        1000,
    )
    return run(
        last_kernel,
        shape(video.shape, bf16),
        (valid, prior_two, double, single, second_double, second_single, columns, rest_two, sums),
        ((early.shape, bf16),),
        1000,
    )


def solution(mesh):
    in_specs = (P("groups", "tm", "rows", None, None), P(), P(), P(), P(), P(), P())
    out_specs = P("groups", "tm", "rows", None, None)
    return jax.shard_map(local, mesh=mesh, in_specs=in_specs, out_specs=out_specs, check_vma=False)
```

```python
import itertools

import jax
import jax.numpy as jnp
from jax import lax
from jax.experimental import pallas as pl
from jax.experimental.pallas import tpu as pltpu
from jax.sharding import PartitionSpec as P

epsilon = 1e-06
VMEM = pl.BlockSpec(memory_space=pltpu.VMEM)
FIRST, LAST = ((0, 1), 3), ((2, 3), 2)


def column(vector_ref):
    row = vector_ref[...].reshape(1, -1)
    count = row.shape[1]
    down = lax.broadcasted_iota(jnp.int32, (count, count), 0)
    across = lax.broadcasted_iota(jnp.int32, (count, count), 1)
    return jnp.sum(jnp.where(down == across, row, 0.0), axis=1, keepdims=True)


def norm_silu(values, gain):
    meansq = jnp.mean(values * values, axis=-2, keepdims=True)
    half = values * lax.rsqrt(meansq + epsilon) * (0.5 * gain)
    return half + half * jnp.tanh(half)


def activate(block, out, gain):
    for frame in range(block.shape[1]):
        for row in range(block.shape[2]):
            values = block[0, frame, row].astype(jnp.float32)
            out[frame, row] = norm_silu(values, gain).astype(jnp.bfloat16)


def restack(weights, offsets, out, lead=()):
    chans = weights.shape[0]
    blank = jnp.zeros((chans, chans), weights.dtype)
    for k in range(3):
        pieces = []
        for offset in offsets:
            if offset is None:
                pieces.append(blank)
            else:
                start = ((offset[0] * 3 + offset[1]) * 3 + k) * chans
                pieces.append(weights[:, start : start + chans])
        out[(*lead, slice(k * chans, (k + 1) * chans), slice(None))] = jnp.concatenate(pieces, axis=1)


def conv(weights, windows):
    columns = [jnp.concatenate(window, axis=0) for window in windows]
    stacked = jnp.dot(weights, jnp.concatenate(columns, axis=1), preferred_element_type=jnp.float32)
    chans, width = windows[0][0].shape
    lane = lax.broadcasted_iota(jnp.int32, (chans, width), 1)
    sums = []
    for index in range(len(windows)):
        part = stacked[:, index * width : (index + 1) * width]
        left = jnp.where(lane == 0, 0.0, pltpu.roll(part[:chans], 1, 1))
        right = jnp.where(lane == width - 1, 0.0, pltpu.roll(part[2 * chans :], width - 1, 1))
        sums.append(part[chans : 2 * chans] + left + right)
    return sums


def four_rows(top):
    return [(top, 0), (top, 1), (1 - top, 0), (1 - top, 1)]


def side_of_one():
    return 1 - lax.rem(lax.axis_index("rows"), 2)


def edge_kernel(valid):
    row_part = lax.axis_index("rows")
    one_below = lax.rem(row_part, 2) == 0
    has_above = row_part > 0
    has_below = row_part < lax.axis_size("rows") - 1
    later = lax.axis_index("tm") > 0
    has_one = (one_below & has_below) | (~one_below & has_above)
    has_two = (one_below & has_above) | (~one_below & has_below)
    for index, flag in enumerate((has_one, has_two, later)):
        valid[index] = jnp.broadcast_to(jnp.where(flag, 1.0, 0.0), valid.shape[1:])


def restack_sides(weights, double, single):
    restack(weights, [(i, j) for i in range(3) for j in (0, 1)], double, (0,))
    restack(weights, [(i, j) for i in range(3) for j in (1, 2)], double, (1,))
    restack(weights, [(i, 0) for i in range(3)], single, (0,))
    restack(weights, [(i, 2) for i in range(3)], single, (1,))


def own_kernel(
    valid, video, gamma_first, kernel_first, bias_first, gamma_second, kernel_second, bias_second,
    own, columns, first, double, single, second_double, second_single, second_12, second_2,
):
    for index, vector in enumerate((gamma_first, bias_first, gamma_second, bias_second)):
        columns[index] = jnp.broadcast_to(column(vector), columns.shape[1:])
    activate(video, own, columns[0])
    weights = kernel_first[...]
    restack(weights, [(i, j) if j < 3 else None for i in range(3) for j in range(4)], first)
    restack_sides(weights, double, single)
    weights = kernel_second[...]
    restack_sides(weights, second_double, second_single)
    restack(weights, [(i, j) for i in (1, 2) for j in range(3)], second_12)
    restack(weights, [(2, j) for j in range(3)], second_2)


def present_frames(cells, side, exists, first, columns, partial, late):
    bias, gain = columns[1], columns[2]
    depth = first.shape[1] // 3
    frames = cells.shape[1]
    rows = four_rows(side)
    for frame in range(frames):
        count = min(frame + 1, 3)
        windows = []
        for row in range(2):
            chosen = rows[row : row + 3] + rows[row + 1 : row + 2]
            windows.append([cells[a, f, r] for f in range(frame + 1 - count, frame + 1) for a, r in chosen])
        sums = conv(first[:, (3 - count) * depth :], windows)
        for row in range(2):
            hidden = sums[row] + bias
            if frame < 2:
                partial[frame, row] = hidden
            else:
                mask = jnp.where(side == row, exists, 1.0)
                late[frame - 2, row] = (norm_silu(hidden, gain) * mask).astype(jnp.bfloat16)


def earlier_sums(double, single, pair, row, group, count):
    frames, _, chans, width = pair.shape
    blank = jnp.zeros((chans, width), pair.dtype)
    depth = 2 * count * chans
    spans = [range(frames - 4 + frame, frames - 4 + frame + count) for frame in group]

    def read(frame, at):
        return pair[frame, at] if frame < frames else blank

    both = conv(double[:, :depth], [[read(f, r) for f in span for r in range(2)] for span in spans])
    alone = conv(single[:, : depth // 2], [[read(f, row) for f in span] for span in spans])
    return list(zip(group, both, alone))


def earlier_rest(double, single, inner, side, partial, bias, rest):
    for group, count in (FIRST, LAST):
        for frame, both, alone in earlier_sums(double.at[1 - side], single.at[1 - side], inner, side, group, count):
            for index, (value, row) in enumerate(((alone, side), (both, 1 - side))):
                rest[frame, index] = value + (bias if frame < 2 else partial[frame - 2, row])


def earlier_frames(sums, side, rest, exists, later, gain, early):
    for frame, both, alone in sums:
        for index, (value, row) in enumerate(((both, side), (alone, 1 - side))):
            value = norm_silu(value * exists + rest[frame, index], gain)
            if index == 0:
                value = value * exists
            if frame < 2:
                value = value * later
            early[frame, row] = value.astype(jnp.bfloat16)


def earlier_result(double, single, near, second_double, second_single, side, rest, exists, later, gain, early):
    sums = earlier_sums(double.at[side], single.at[side], near, 1 - side, *LAST)
    earlier_frames(sums, side, rest, exists, later, gain, early)
    sums = earlier_sums(double.at[side], single.at[side], near, 1 - side, *FIRST)
    result = earlier_sums(second_double.at[side], second_single.at[side], early, 1 - side, *LAST)
    earlier_frames(sums, side, rest, exists, later, gain, early)
    return result + earlier_sums(second_double.at[side], second_single.at[side], early, 1 - side, *FIRST)


def one_kernel(valid, one, own, first, columns, partial, late, cells):
    activate(one, cells.at[0], columns[0] * valid[0, 0:1])
    cells[1] = own[...]
    present_frames(cells, side_of_one(), valid[0, 0:1], first, columns, partial, late)


def two_kernel(
    partial_one, late_one, valid, two, inner, own, first, double, single, second_12, second_2, columns,
    rest_one, rest_two, late_sums, cells, partial, late,
):
    side = side_of_one()
    activate(two, cells.at[0], columns[0] * valid[1, 0:1])
    cells[1] = own[...]
    late[0] = late_one[...]
    present_frames(cells, 1 - side, valid[1, 0:1], first, columns, partial, late.at[1])
    earlier_rest(double, single, inner, side, partial_one, columns[1], rest_one)
    earlier_rest(double, single, inner, 1 - side, partial, columns[1], rest_two)
    rows = four_rows(side)
    for frame, weights in ((0, second_2), (1, second_12)):
        windows = [[late[a, f, r] for f in range(frame + 1) for a, r in rows[row : row + 3]] for row in range(2)]
        for row, value in enumerate(conv(weights[...], windows)):
            late_sums[frame, row] = value + columns[3]


def inner_kernel(valid, prior, columns, inner):
    activate(prior, inner, columns[0] * valid[2, 0:1])


def prior_kernel(
    valid, video, near, double, single, second_double, second_single, columns, rest, late_sums, sums, early
):
    side = side_of_one()
    result = earlier_result(
        double, single, near, second_double, second_single, side, rest, valid[0, 0:1], valid[2, 0:1], columns[2], early
    )
    for frame, both, alone in result:
        for value, row in ((both, side), (alone, 1 - side)):
            rest_of_sum = columns[3] if frame < 2 else late_sums[frame - 2, row]
            sums[frame, row] = video[0, frame, row].astype(jnp.float32) + (value + rest_of_sum)


def last_kernel(
    valid, near, double, single, second_double, second_single, columns, rest, sums, encoded, early, near_sums
):
    side = 1 - side_of_one()
    has_earlier = lax.axis_index("tm") > 0

    @pl.when(has_earlier)
    def _():
        for group, count in (LAST, FIRST):
            for frame, both, alone in earlier_sums(double.at[side], single.at[side], near, 1 - side, group, count):
                near_sums[frame, 0] = both
                near_sums[frame, 1] = alone

    @pl.when(~has_earlier)
    def _():
        near_sums[...] = jnp.zeros_like(near_sums)

    result = []
    for group, count in (LAST, FIRST):
        parts = [(frame, near_sums[frame, 0], near_sums[frame, 1]) for frame in group]
        earlier_frames(parts, side, rest, valid[1, 0:1], valid[2, 0:1], columns[2], early)
        result += earlier_sums(second_double.at[side], second_single.at[side], early, 1 - side, group, count)
    for frame, both, alone in result:
        for value, row in ((both, side), (alone, 1 - side)):
            encoded[0, frame, row] = (sums[frame, row] + value).astype(jnp.bfloat16)


def routed(block, goal):
    sizes = [lax.axis_size(axis) for axis in ("groups", "rows", "tm")]
    places = list(itertools.product(*map(range, sizes)))
    route = [(index, places.index(goal(place, sizes))) for index, place in enumerate(places)]
    return lax.ppermute(block, ("groups", "rows", "tm"), route)


def later(place, sizes):
    group, row, part = place
    return group, row, (part + 1) % sizes[2]


def paired(place, sizes, partner):
    group, row, part = place
    if 0 <= partner < sizes[1]:
        return group, partner, part
    return group, row, min(part ^ 1, sizes[2] - 1)


def even_pair(place, sizes):
    return paired(place, sizes, place[1] + 1 - 2 * (place[1] % 2))


def odd_pair(place, sizes):
    return paired(place, sizes, place[1] - 1 + 2 * (place[1] % 2))


def if_earlier(pair):
    def goal(place, sizes):
        group, row, part = place
        if part == 0 and pair(place, sizes)[1] != row and group ^ 1 < sizes[0]:
            return group ^ 1, row, part
        return pair(place, sizes)

    return goal


def local(video, gamma_first, kernel_first, bias_first, gamma_second, kernel_second, bias_second):
    _, frames, rows, chans, width = video.shape
    assert frames == 4 and rows == 2
    prior = routed(video, later)
    two = routed(video, odd_pair)
    one = routed(video, even_pair)
    bf16, f32 = jnp.bfloat16, jnp.float32
    shape = jax.ShapeDtypeStruct
    params = pltpu.CompilerParams(vmem_limit_bytes=24 * 2**20)

    def run(kernel, out_shape, operands, scratch=(), millions=1000):
        single_out = not isinstance(out_shape, tuple)
        return pl.pallas_call(
            kernel,
            out_shape=out_shape,
            in_specs=[VMEM] * len(operands),
            out_specs=VMEM if single_out else [VMEM] * len(out_shape),
            scratch_shapes=[pltpu.VMEM(*one_scratch) for one_scratch in scratch],
            compiler_params=params,
            cost_estimate=pl.CostEstimate(flops=millions * 10**6, bytes_accessed=10**6, transcendentals=10**5),
        )(*operands)

    def stacked(*lead_and_taps):
        *lead, taps = lead_and_taps
        return shape((*lead, 3 * chans, taps * chans), bf16)

    block = (frames, rows, chans, width)
    cells = ((2, *block), bf16)
    pair = shape((2, 2, chans, width), f32)
    late = shape((2, 2, chans, width), bf16)
    rest = shape((4, 2, chans, width), f32)
    early = shape((4, 2, chans, width), bf16)
    valid = run(edge_kernel, shape((3, 8, width), f32), (), millions=2000)
    own, columns, first, double, single, second_double, second_single, second_12, second_2 = run(
        own_kernel,
        (
            shape(block, bf16),
            shape((4, chans, width), f32),
            *(stacked(12), stacked(2, 6), stacked(2, 3), stacked(2, 6), stacked(2, 3), stacked(6), stacked(3)),
        ),
        (valid, video, gamma_first, kernel_first, bias_first, gamma_second, kernel_second, bias_second),
        millions=10,
    )
    inner = run(inner_kernel, shape(block, bf16), (valid, prior, columns), millions=10)
    prior_two = routed(inner, if_earlier(odd_pair))
    prior_one = routed(inner, if_earlier(even_pair))
    partial_one, late_one = run(one_kernel, (pair, late), (valid, one, own, first, columns), (cells,), 10)
    rest_one, rest_two, late_sums = run(
        two_kernel,
        (rest, rest, pair),
        (partial_one, late_one, valid, two, inner, own, first, double, single, second_12, second_2, columns),
        (cells, (pair.shape, f32), ((2, *late.shape), bf16)),
        10,
    )
    sums = run(
        prior_kernel,
        rest,
        (valid, video, prior_one, double, single, second_double, second_single, columns, rest_one, late_sums),
        ((early.shape, bf16),),
        1000,
    )
    return run(
        last_kernel,
        shape(video.shape, bf16),
        (valid, prior_two, double, single, second_double, second_single, columns, rest_two, sums),
        ((early.shape, bf16), (rest.shape, f32)),
        1000,
    )


def solution(mesh):
    in_specs = (P("groups", "tm", "rows", None, None), P(), P(), P(), P(), P(), P())
    out_specs = P("groups", "tm", "rows", None, None)
    return jax.shard_map(local, mesh=mesh, in_specs=in_specs, out_specs=out_specs, check_vma=False)
```

```python
import itertools

import jax
import jax.numpy as jnp
from jax import lax
from jax.experimental import pallas as pl
from jax.experimental.pallas import tpu as pltpu
from jax.sharding import PartitionSpec as P

epsilon = 1e-06
VMEM = pl.BlockSpec(memory_space=pltpu.VMEM)
FIRST, LAST = ((0, 1), 3), ((2, 3), 2)


def column(vector_ref):
    row = vector_ref[...].reshape(1, -1)
    count = row.shape[1]
    down = lax.broadcasted_iota(jnp.int32, (count, count), 0)
    across = lax.broadcasted_iota(jnp.int32, (count, count), 1)
    return jnp.sum(jnp.where(down == across, row, 0.0), axis=1, keepdims=True)


def norm_silu(values, gain):
    meansq = jnp.mean(values * values, axis=-2, keepdims=True)
    half = values * lax.rsqrt(meansq + epsilon) * (0.5 * gain)
    return half + half * jnp.tanh(half)


def activate(block, out, gain):
    for frame in range(block.shape[1]):
        for row in range(block.shape[2]):
            values = block[0, frame, row].astype(jnp.float32)
            out[frame, row] = norm_silu(values, gain).astype(jnp.bfloat16)


def restack(weights, offsets, out, lead=()):
    chans = weights.shape[0]
    blank = jnp.zeros((chans, chans), weights.dtype)
    for k in range(3):
        pieces = []
        for offset in offsets:
            if offset is None:
                pieces.append(blank)
            else:
                start = ((offset[0] * 3 + offset[1]) * 3 + k) * chans
                pieces.append(weights[:, start : start + chans])
        out[(*lead, slice(k * chans, (k + 1) * chans), slice(None))] = jnp.concatenate(pieces, axis=1)


def conv(weights, windows):
    columns = [jnp.concatenate(window, axis=0) for window in windows]
    stacked = jnp.dot(weights, jnp.concatenate(columns, axis=1), preferred_element_type=jnp.float32)
    chans, width = windows[0][0].shape
    lane = lax.broadcasted_iota(jnp.int32, (chans, width), 1)
    sums = []
    for index in range(len(windows)):
        part = stacked[:, index * width : (index + 1) * width]
        left = jnp.where(lane == 0, 0.0, pltpu.roll(part[:chans], 1, 1))
        right = jnp.where(lane == width - 1, 0.0, pltpu.roll(part[2 * chans :], width - 1, 1))
        sums.append(part[chans : 2 * chans] + left + right)
    return sums


def four_rows(top):
    return [(top, 0), (top, 1), (1 - top, 0), (1 - top, 1)]


def side_of_one():
    return 1 - lax.rem(lax.axis_index("rows"), 2)


def edge_kernel(valid):
    row_part = lax.axis_index("rows")
    one_below = lax.rem(row_part, 2) == 0
    has_above = row_part > 0
    has_below = row_part < lax.axis_size("rows") - 1
    later = lax.axis_index("tm") > 0
    has_one = (one_below & has_below) | (~one_below & has_above)
    has_two = (one_below & has_above) | (~one_below & has_below)
    for index, flag in enumerate((has_one, has_two, later)):
        valid[index] = jnp.broadcast_to(jnp.where(flag, 1.0, 0.0), valid.shape[1:])


def restack_sides(weights, double, single):
    restack(weights, [(i, j) for i in range(3) for j in (0, 1)], double, (0,))
    restack(weights, [(i, j) for i in range(3) for j in (1, 2)], double, (1,))
    restack(weights, [(i, 0) for i in range(3)], single, (0,))
    restack(weights, [(i, 2) for i in range(3)], single, (1,))


def own_kernel(
    valid, video, gamma_first, kernel_first, bias_first, gamma_second, kernel_second, bias_second,
    own, columns, first, double, single, second_double, second_single, second_12, second_2,
):
    for index, vector in enumerate((gamma_first, bias_first, gamma_second, bias_second)):
        columns[index] = jnp.broadcast_to(column(vector), columns.shape[1:])
    activate(video, own, columns[0])
    weights = kernel_first[...]
    restack(weights, [(i, j) if j < 3 else None for i in range(3) for j in range(4)], first)
    restack_sides(weights, double, single)
    weights = kernel_second[...]
    restack_sides(weights, second_double, second_single)
    restack(weights, [(i, j) for i in (1, 2) for j in range(3)], second_12)
    restack(weights, [(2, j) for j in range(3)], second_2)


def present_frames(cells, side, exists, first, columns, partial, late):
    bias, gain = columns[1], columns[2]
    depth = first.shape[1] // 3
    frames = cells.shape[1]
    rows = four_rows(side)
    for frame in range(frames):
        count = min(frame + 1, 3)
        windows = []
        for row in range(2):
            chosen = rows[row : row + 3] + rows[row + 1 : row + 2]
            windows.append([cells[a, f, r] for f in range(frame + 1 - count, frame + 1) for a, r in chosen])
        sums = conv(first[:, (3 - count) * depth :], windows)
        for row in range(2):
            hidden = sums[row] + bias
            if frame < 2:
                partial[frame, row] = hidden
            else:
                mask = jnp.where(side == row, exists, 1.0)
                late[frame - 2, row] = (norm_silu(hidden, gain) * mask).astype(jnp.bfloat16)


def earlier_sums(double, single, pair, row, group, count):
    frames, _, chans, width = pair.shape
    blank = jnp.zeros((chans, width), pair.dtype)
    depth = 2 * count * chans
    spans = [range(frames - 4 + frame, frames - 4 + frame + count) for frame in group]

    def read(frame, at):
        return pair[frame, at] if frame < frames else blank

    both = conv(double[:, :depth], [[read(f, r) for f in span for r in range(2)] for span in spans])
    alone = conv(single[:, : depth // 2], [[read(f, row) for f in span] for span in spans])
    return list(zip(group, both, alone))


def earlier_rest(double, single, inner, side, partial, bias, rest):
    for group, count in (FIRST, LAST):
        for frame, both, alone in earlier_sums(double.at[1 - side], single.at[1 - side], inner, side, group, count):
            for index, (value, row) in enumerate(((alone, side), (both, 1 - side))):
                rest[frame, index] = value + (bias if frame < 2 else partial[frame - 2, row])


def earlier_frames(sums, side, rest, exists, later, gain, early):
    for frame, both, alone in sums:
        for index, (value, row) in enumerate(((both, side), (alone, 1 - side))):
            value = norm_silu(value * exists + rest[frame, index], gain)
            if index == 0:
                value = value * exists
            if frame < 2:
                value = value * later
            early[frame, row] = value.astype(jnp.bfloat16)


def earlier_result(double, single, near, second_double, second_single, side, rest, exists, later, gain, early):
    sums = earlier_sums(double.at[side], single.at[side], near, 1 - side, *LAST)
    earlier_frames(sums, side, rest, exists, later, gain, early)
    sums = earlier_sums(double.at[side], single.at[side], near, 1 - side, *FIRST)
    result = earlier_sums(second_double.at[side], second_single.at[side], early, 1 - side, *LAST)
    earlier_frames(sums, side, rest, exists, later, gain, early)
    return result + earlier_sums(second_double.at[side], second_single.at[side], early, 1 - side, *FIRST)


def one_kernel(valid, one, own, first, columns, partial, late, cells):
    activate(one, cells.at[0], columns[0] * valid[0, 0:1])
    cells[1] = own[...]
    present_frames(cells, side_of_one(), valid[0, 0:1], first, columns, partial, late)


def two_kernel(
    partial_one, late_one, valid, two, inner, own, first, double, single, second_12, second_2, columns,
    rest_one, rest_two, late_sums, cells, partial, late,
):
    side = side_of_one()
    activate(two, cells.at[0], columns[0] * valid[1, 0:1])
    cells[1] = own[...]
    late[0] = late_one[...]
    present_frames(cells, 1 - side, valid[1, 0:1], first, columns, partial, late.at[1])
    earlier_rest(double, single, inner, side, partial_one, columns[1], rest_one)
    earlier_rest(double, single, inner, 1 - side, partial, columns[1], rest_two)
    rows = four_rows(side)
    for frame, weights in ((0, second_2), (1, second_12)):
        windows = [[late[a, f, r] for f in range(frame + 1) for a, r in rows[row : row + 3]] for row in range(2)]
        for row, value in enumerate(conv(weights[...], windows)):
            late_sums[frame, row] = value + columns[3]


def inner_kernel(valid, prior, columns, inner):
    activate(prior, inner, columns[0] * valid[2, 0:1])


def prior_kernel(
    valid, video, near, double, single, second_double, second_single, columns, rest, late_sums, sums, early
):
    side = side_of_one()
    result = earlier_result(
        double, single, near, second_double, second_single, side, rest, valid[0, 0:1], valid[2, 0:1], columns[2], early
    )
    for frame, both, alone in result:
        for value, row in ((both, side), (alone, 1 - side)):
            rest_of_sum = columns[3] if frame < 2 else late_sums[frame - 2, row]
            sums[frame, row] = video[0, frame, row].astype(jnp.float32) + (value + rest_of_sum)


def last_kernel(
    valid, near, double, single, second_double, second_single, columns, rest, sums, encoded, early, near_sums, ready, sems
):
    side = 1 - side_of_one()
    has_earlier = lax.axis_index("tm") > 0

    @pl.when(has_earlier)
    def _():
        for group, count in (LAST, FIRST):
            for frame, both, alone in earlier_sums(double.at[side], single.at[side], near, 1 - side, group, count):
                near_sums[frame, 0] = both
                near_sums[frame, 1] = alone

    @pl.when(~has_earlier)
    def _():
        near_sums[...] = jnp.zeros_like(near_sums)

    moves = []
    for group, count in (LAST, FIRST):
        parts = [(frame, near_sums[frame, 0], near_sums[frame, 1]) for frame in group]
        earlier_frames(parts, side, rest, valid[1, 0:1], valid[2, 0:1], columns[2], early)
        result = earlier_sums(second_double.at[side], second_single.at[side], early, 1 - side, group, count)
        for frame, both, alone in result:
            for value, row in ((both, side), (alone, 1 - side)):
                ready[0, frame, row] = (sums[frame, row] + value).astype(jnp.bfloat16)
        chosen = (0, slice(group[0], group[-1] + 1))
        move = pltpu.make_async_copy(ready.at[chosen], encoded.at[chosen], sems.at[len(moves)])
        move.start()
        moves.append(move)
    for move in moves:
        move.wait()


def routed(block, goal):
    sizes = [lax.axis_size(axis) for axis in ("groups", "rows", "tm")]
    places = list(itertools.product(*map(range, sizes)))
    route = [(index, places.index(goal(place, sizes))) for index, place in enumerate(places)]
    return lax.ppermute(block, ("groups", "rows", "tm"), route)


def later(place, sizes):
    group, row, part = place
    return group, row, (part + 1) % sizes[2]


def paired(place, sizes, partner):
    group, row, part = place
    if 0 <= partner < sizes[1]:
        return group, partner, part
    return group, row, min(part ^ 1, sizes[2] - 1)


def even_pair(place, sizes):
    return paired(place, sizes, place[1] + 1 - 2 * (place[1] % 2))


def odd_pair(place, sizes):
    return paired(place, sizes, place[1] - 1 + 2 * (place[1] % 2))


def if_earlier(pair):
    def goal(place, sizes):
        group, row, part = place
        if part == 0 and pair(place, sizes)[1] != row and group ^ 1 < sizes[0]:
            return group ^ 1, row, part
        return pair(place, sizes)

    return goal


def local(video, gamma_first, kernel_first, bias_first, gamma_second, kernel_second, bias_second):
    _, frames, rows, chans, width = video.shape
    assert frames == 4 and rows == 2
    prior = routed(video, later)
    two = routed(video, odd_pair)
    one = routed(video, even_pair)
    bf16, f32 = jnp.bfloat16, jnp.float32
    shape = jax.ShapeDtypeStruct
    params = pltpu.CompilerParams(vmem_limit_bytes=24 * 2**20)

    def run(kernel, out_shape, operands, scratch=(), millions=1000, out_spec=VMEM, sems=()):
        single_out = not isinstance(out_shape, tuple)
        return pl.pallas_call(
            kernel,
            out_shape=out_shape,
            in_specs=[VMEM] * len(operands),
            out_specs=out_spec if single_out else [VMEM] * len(out_shape),
            scratch_shapes=[pltpu.VMEM(*one_scratch) for one_scratch in scratch] + list(sems),
            compiler_params=params,
            cost_estimate=pl.CostEstimate(flops=millions * 10**6, bytes_accessed=10**6, transcendentals=10**5),
        )(*operands)

    def stacked(*lead_and_taps):
        *lead, taps = lead_and_taps
        return shape((*lead, 3 * chans, taps * chans), bf16)

    block = (frames, rows, chans, width)
    cells = ((2, *block), bf16)
    pair = shape((2, 2, chans, width), f32)
    late = shape((2, 2, chans, width), bf16)
    rest = shape((4, 2, chans, width), f32)
    early = shape((4, 2, chans, width), bf16)
    valid = run(edge_kernel, shape((3, 8, width), f32), (), millions=2000)
    own, columns, first, double, single, second_double, second_single, second_12, second_2 = run(
        own_kernel,
        (
            shape(block, bf16),
            shape((4, chans, width), f32),
            *(stacked(12), stacked(2, 6), stacked(2, 3), stacked(2, 6), stacked(2, 3), stacked(6), stacked(3)),
        ),
        (valid, video, gamma_first, kernel_first, bias_first, gamma_second, kernel_second, bias_second),
        millions=10,
    )
    inner = run(inner_kernel, shape(block, bf16), (valid, prior, columns), millions=10)
    prior_two = routed(inner, if_earlier(odd_pair))
    prior_one = routed(inner, if_earlier(even_pair))
    partial_one, late_one = run(one_kernel, (pair, late), (valid, one, own, first, columns), (cells,), 10)
    rest_one, rest_two, late_sums = run(
        two_kernel,
        (rest, rest, pair),
        (partial_one, late_one, valid, two, inner, own, first, double, single, second_12, second_2, columns),
        (cells, (pair.shape, f32), ((2, *late.shape), bf16)),
        10,
    )
    sums = run(
        prior_kernel,
        rest,
        (valid, video, prior_one, double, single, second_double, second_single, columns, rest_one, late_sums),
        ((early.shape, bf16),),
        1000,
    )
    return run(
        last_kernel,
        shape(video.shape, bf16),
        (valid, prior_two, double, single, second_double, second_single, columns, rest_two, sums),
        ((early.shape, bf16), (rest.shape, f32), (video.shape, bf16)),
        1000,
        pl.BlockSpec(memory_space=pl.ANY),
        [pltpu.SemaphoreType.DMA((2,))],
    )


def solution(mesh):
    in_specs = (P("groups", "tm", "rows", None, None), P(), P(), P(), P(), P(), P())
    out_specs = P("groups", "tm", "rows", None, None)
    return jax.shard_map(local, mesh=mesh, in_specs=in_specs, out_specs=out_specs, check_vma=False)
```

```python
import itertools

import jax
import jax.numpy as jnp
from jax import lax
from jax.experimental import pallas as pl
from jax.experimental.pallas import tpu as pltpu
from jax.sharding import PartitionSpec as P

epsilon = 1e-06
VMEM = pl.BlockSpec(memory_space=pltpu.VMEM)
FIRST, LAST = ((0, 1), 3), ((2, 3), 2)


def column(vector_ref):
    row = vector_ref[...].reshape(1, -1)
    count = row.shape[1]
    down = lax.broadcasted_iota(jnp.int32, (count, count), 0)
    across = lax.broadcasted_iota(jnp.int32, (count, count), 1)
    return jnp.sum(jnp.where(down == across, row, 0.0), axis=1, keepdims=True)


def norm_silu(values, gain):
    meansq = jnp.mean(values * values, axis=-2, keepdims=True)
    half = values * lax.rsqrt(meansq + epsilon) * (0.5 * gain)
    return half + half * jnp.tanh(half)


def activate(block, out, gain):
    for frame in range(block.shape[1]):
        for row in range(block.shape[2]):
            values = block[0, frame, row].astype(jnp.float32)
            out[frame, row] = norm_silu(values, gain).astype(jnp.bfloat16)


def restack(weights, offsets, out, lead=()):
    chans = weights.shape[0]
    blank = jnp.zeros((chans, chans), weights.dtype)
    for k in range(3):
        pieces = []
        for offset in offsets:
            if offset is None:
                pieces.append(blank)
            else:
                start = ((offset[0] * 3 + offset[1]) * 3 + k) * chans
                pieces.append(weights[:, start : start + chans])
        out[(*lead, slice(k * chans, (k + 1) * chans), slice(None))] = jnp.concatenate(pieces, axis=1)


def conv(weights, windows):
    columns = [jnp.concatenate(window, axis=0) for window in windows]
    stacked = jnp.dot(weights, jnp.concatenate(columns, axis=1), preferred_element_type=jnp.float32)
    chans, width = windows[0][0].shape
    lane = lax.broadcasted_iota(jnp.int32, (chans, width), 1)
    sums = []
    for index in range(len(windows)):
        part = stacked[:, index * width : (index + 1) * width]
        left = jnp.where(lane == 0, 0.0, pltpu.roll(part[:chans], 1, 1))
        right = jnp.where(lane == width - 1, 0.0, pltpu.roll(part[2 * chans :], width - 1, 1))
        sums.append(part[chans : 2 * chans] + left + right)
    return sums


def four_rows(top):
    return [(top, 0), (top, 1), (1 - top, 0), (1 - top, 1)]


def side_of_one():
    return 1 - lax.rem(lax.axis_index("rows"), 2)


def edge_kernel(valid):
    row_part = lax.axis_index("rows")
    one_below = lax.rem(row_part, 2) == 0
    has_above = row_part > 0
    has_below = row_part < lax.axis_size("rows") - 1
    later = lax.axis_index("tm") > 0
    has_one = (one_below & has_below) | (~one_below & has_above)
    has_two = (one_below & has_above) | (~one_below & has_below)
    for index, flag in enumerate((has_one, has_two, later)):
        valid[index] = jnp.broadcast_to(jnp.where(flag, 1.0, 0.0), valid.shape[1:])


def restack_sides(weights, double, single):
    restack(weights, [(i, j) for i in range(3) for j in (0, 1)], double, (0,))
    restack(weights, [(i, j) for i in range(3) for j in (1, 2)], double, (1,))
    restack(weights, [(i, 0) for i in range(3)], single, (0,))
    restack(weights, [(i, 2) for i in range(3)], single, (1,))


def own_kernel(
    valid, video, gamma_first, kernel_first, bias_first, gamma_second, kernel_second, bias_second,
    own, columns, first, double, single, second_double, second_single, second_12, second_2,
):
    for index, vector in enumerate((gamma_first, bias_first, gamma_second, bias_second)):
        columns[index] = jnp.broadcast_to(column(vector), columns.shape[1:])
    activate(video, own, columns[0])
    weights = kernel_first[...]
    restack(weights, [(i, j) if j < 3 else None for i in range(3) for j in range(4)], first)
    restack_sides(weights, double, single)
    weights = kernel_second[...]
    restack_sides(weights, second_double, second_single)
    restack(weights, [(i, j) for i in (1, 2) for j in range(3)], second_12)
    restack(weights, [(2, j) for j in range(3)], second_2)


def present_frames(cells, side, exists, first, columns, partial, late):
    bias, gain = columns[1], columns[2]
    depth = first.shape[1] // 3
    frames = cells.shape[1]
    rows = four_rows(side)
    for frame in range(frames):
        count = min(frame + 1, 3)
        windows = []
        for row in range(2):
            chosen = rows[row : row + 3] + rows[row + 1 : row + 2]
            windows.append([cells[a, f, r] for f in range(frame + 1 - count, frame + 1) for a, r in chosen])
        sums = conv(first[:, (3 - count) * depth :], windows)
        for row in range(2):
            hidden = sums[row] + bias
            if frame < 2:
                partial[frame, row] = hidden
            else:
                mask = jnp.where(side == row, exists, 1.0)
                late[frame - 2, row] = (norm_silu(hidden, gain) * mask).astype(jnp.bfloat16)


def earlier_sums(double, single, pair, row, group, count):
    frames, _, chans, width = pair.shape
    blank = jnp.zeros((chans, width), pair.dtype)
    depth = 2 * count * chans
    spans = [range(frames - 4 + frame, frames - 4 + frame + count) for frame in group]

    def read(frame, at):
        return pair[frame, at] if frame < frames else blank

    both = conv(double[:, :depth], [[read(f, r) for f in span for r in range(2)] for span in spans])
    alone = conv(single[:, : depth // 2], [[read(f, row) for f in span] for span in spans])
    return list(zip(group, both, alone))


def earlier_rest(double, single, inner, side, partial, bias, rest):
    for group, count in (FIRST, LAST):
        for frame, both, alone in earlier_sums(double.at[1 - side], single.at[1 - side], inner, side, group, count):
            for index, (value, row) in enumerate(((alone, side), (both, 1 - side))):
                rest[frame, index] = value + (bias if frame < 2 else partial[frame - 2, row])


def earlier_frames(sums, side, rest, exists, later, gain, early):
    for frame, both, alone in sums:
        for index, (value, row) in enumerate(((both, side), (alone, 1 - side))):
            value = norm_silu(value * exists + rest[frame, index], gain)
            if index == 0:
                value = value * exists
            if frame < 2:
                value = value * later
            early[frame, row] = value.astype(jnp.bfloat16)


def earlier_result(double, single, near, second_double, second_single, side, rest, exists, later, gain, early):
    sums = earlier_sums(double.at[side], single.at[side], near, 1 - side, *LAST)
    earlier_frames(sums, side, rest, exists, later, gain, early)
    sums = earlier_sums(double.at[side], single.at[side], near, 1 - side, *FIRST)
    result = earlier_sums(second_double.at[side], second_single.at[side], early, 1 - side, *LAST)
    earlier_frames(sums, side, rest, exists, later, gain, early)
    return result + earlier_sums(second_double.at[side], second_single.at[side], early, 1 - side, *FIRST)


def one_kernel(valid, one, own, first, columns, partial, late, cells):
    activate(one, cells.at[0], columns[0] * valid[0, 0:1])
    cells[1] = own[...]
    present_frames(cells, side_of_one(), valid[0, 0:1], first, columns, partial, late)


def two_kernel(
    partial_one, late_one, valid, two, inner, own, first, double, single, second_12, second_2, columns,
    rest_one, rest_two, late_sums, cells, partial, late,
):
    side = side_of_one()
    activate(two, cells.at[0], columns[0] * valid[1, 0:1])
    cells[1] = own[...]
    late[0] = late_one[...]
    present_frames(cells, 1 - side, valid[1, 0:1], first, columns, partial, late.at[1])
    earlier_rest(double, single, inner, side, partial_one, columns[1], rest_one)
    earlier_rest(double, single, inner, 1 - side, partial, columns[1], rest_two)
    rows = four_rows(side)
    for frame, weights in ((0, second_2), (1, second_12)):
        windows = [[late[a, f, r] for f in range(frame + 1) for a, r in rows[row : row + 3]] for row in range(2)]
        for row, value in enumerate(conv(weights[...], windows)):
            late_sums[frame, row] = value + columns[3]


def inner_kernel(valid, prior, columns, inner):
    activate(prior, inner, columns[0] * valid[2, 0:1])


def prior_kernel(
    valid, video, near, double, single, second_double, second_single, columns, rest, late_sums, sums, early
):
    side = side_of_one()
    result = earlier_result(
        double, single, near, second_double, second_single, side, rest, valid[0, 0:1], valid[2, 0:1], columns[2], early
    )
    for frame, both, alone in result:
        for value, row in ((both, side), (alone, 1 - side)):
            rest_of_sum = columns[3] if frame < 2 else late_sums[frame - 2, row]
            sums[frame, row] = video[0, frame, row].astype(jnp.float32) + (value + rest_of_sum)


def last_kernel(
    valid, near, double, single, second_double, second_single, columns, rest, sums, encoded, early, near_sums, ready, sems
):
    side = 1 - side_of_one()
    row_part, row_parts = lax.axis_index("rows"), lax.axis_size("rows")
    has_two = (row_part > 0) & ((row_part < row_parts - 1) | (row_parts % 2 == 1))
    has_earlier = (lax.axis_index("tm") > 0) & has_two

    @pl.when(has_earlier)
    def _():
        for group, count in (LAST, FIRST):
            for frame, both, alone in earlier_sums(double.at[side], single.at[side], near, 1 - side, group, count):
                near_sums[frame, 0] = both
                near_sums[frame, 1] = alone

    @pl.when(~has_earlier)
    def _():
        near_sums[...] = jnp.zeros_like(near_sums)

    moves = []
    for group, count in (LAST, FIRST):
        parts = [(frame, near_sums[frame, 0], near_sums[frame, 1]) for frame in group]
        earlier_frames(parts, side, rest, valid[1, 0:1], valid[2, 0:1], columns[2], early)
        result = earlier_sums(second_double.at[side], second_single.at[side], early, 1 - side, group, count)
        for frame, both, alone in result:
            for value, row in ((both, side), (alone, 1 - side)):
                ready[0, frame, row] = (sums[frame, row] + value).astype(jnp.bfloat16)
        chosen = (0, slice(group[0], group[-1] + 1))
        move = pltpu.make_async_copy(ready.at[chosen], encoded.at[chosen], sems.at[len(moves)])
        move.start()
        moves.append(move)
    for move in moves:
        move.wait()


def routed(block, goal):
    sizes = [lax.axis_size(axis) for axis in ("groups", "rows", "tm")]
    places = list(itertools.product(*map(range, sizes)))
    route = [(index, places.index(goal(place, sizes))) for index, place in enumerate(places)]
    return lax.ppermute(block, ("groups", "rows", "tm"), route)


def later(place, sizes):
    group, row, part = place
    return group, row, (part + 1) % sizes[2]


def paired(place, sizes, partner):
    group, row, part = place
    if 0 <= partner < sizes[1]:
        return group, partner, part
    return group, row, min(part ^ 1, sizes[2] - 1)


def even_pair(place, sizes):
    return paired(place, sizes, place[1] + 1 - 2 * (place[1] % 2))


def odd_pair(place, sizes):
    return paired(place, sizes, place[1] - 1 + 2 * (place[1] % 2))


def if_earlier(pair):
    def goal(place, sizes):
        group, row, part = place
        if part == 0 and pair(place, sizes)[1] != row and group ^ 1 < sizes[0]:
            return group ^ 1, row, part
        return pair(place, sizes)

    return goal


def local(video, gamma_first, kernel_first, bias_first, gamma_second, kernel_second, bias_second):
    _, frames, rows, chans, width = video.shape
    assert frames == 4 and rows == 2
    prior = routed(video, later)
    two = routed(video, odd_pair)
    one = routed(video, even_pair)
    bf16, f32 = jnp.bfloat16, jnp.float32
    shape = jax.ShapeDtypeStruct
    params = pltpu.CompilerParams(vmem_limit_bytes=24 * 2**20)

    def run(kernel, out_shape, operands, scratch=(), millions=1000, out_spec=VMEM, sems=()):
        single_out = not isinstance(out_shape, tuple)
        return pl.pallas_call(
            kernel,
            out_shape=out_shape,
            in_specs=[VMEM] * len(operands),
            out_specs=out_spec if single_out else [VMEM] * len(out_shape),
            scratch_shapes=[pltpu.VMEM(*one_scratch) for one_scratch in scratch] + list(sems),
            compiler_params=params,
            cost_estimate=pl.CostEstimate(flops=millions * 10**6, bytes_accessed=10**6, transcendentals=10**5),
        )(*operands)

    def stacked(*lead_and_taps):
        *lead, taps = lead_and_taps
        return shape((*lead, 3 * chans, taps * chans), bf16)

    block = (frames, rows, chans, width)
    cells = ((2, *block), bf16)
    pair = shape((2, 2, chans, width), f32)
    late = shape((2, 2, chans, width), bf16)
    rest = shape((4, 2, chans, width), f32)
    early = shape((4, 2, chans, width), bf16)
    valid = run(edge_kernel, shape((3, 8, width), f32), (), millions=2000)
    own, columns, first, double, single, second_double, second_single, second_12, second_2 = run(
        own_kernel,
        (
            shape(block, bf16),
            shape((4, chans, width), f32),
            *(stacked(12), stacked(2, 6), stacked(2, 3), stacked(2, 6), stacked(2, 3), stacked(6), stacked(3)),
        ),
        (valid, video, gamma_first, kernel_first, bias_first, gamma_second, kernel_second, bias_second),
        millions=10,
    )
    inner = run(inner_kernel, shape(block, bf16), (valid, prior, columns), millions=10)
    prior_two = routed(inner, if_earlier(odd_pair))
    prior_one = routed(inner, if_earlier(even_pair))
    partial_one, late_one = run(one_kernel, (pair, late), (valid, one, own, first, columns), (cells,), 10)
    rest_one, rest_two, late_sums = run(
        two_kernel,
        (rest, rest, pair),
        (partial_one, late_one, valid, two, inner, own, first, double, single, second_12, second_2, columns),
        (cells, (pair.shape, f32), ((2, *late.shape), bf16)),
        10,
    )
    sums = run(
        prior_kernel,
        rest,
        (valid, video, prior_one, double, single, second_double, second_single, columns, rest_one, late_sums),
        ((early.shape, bf16),),
        1000,
    )
    return run(
        last_kernel,
        shape(video.shape, bf16),
        (valid, prior_two, double, single, second_double, second_single, columns, rest_two, sums),
        ((early.shape, bf16), (rest.shape, f32), (video.shape, bf16)),
        1000,
        pl.BlockSpec(memory_space=pl.ANY),
        [pltpu.SemaphoreType.DMA((2,))],
    )


def solution(mesh):
    in_specs = (P("groups", "tm", "rows", None, None), P(), P(), P(), P(), P(), P())
    out_specs = P("groups", "tm", "rows", None, None)
    return jax.shard_map(local, mesh=mesh, in_specs=in_specs, out_specs=out_specs, check_vma=False)
```
